32 devices in a mesh: section: 4 (over y, x), dp: 8 (over z, core).
Axes of the slice: x: 2, y: 2, z: 4, core: 2. Of those that a mesh axis runs over, the one named last changes fastest.
Arguments:
- inputs_x: bfloat16 [2, 8, 512, 1024], P(None, 'dp'), may hold values from -6 to 6
- lengths: int32 [2, 8], P(None, 'dp'), may hold values from 128 to 512, as said below
- w_main: bfloat16 [4, 1024, 4096], P('section')
- w_down: bfloat16 [2, 4096, 1024], replicated, may hold values from -0.09375 to 0.09375
- gains: float32 [4, 1024], P('section'), may hold values from 0.5 to 1.5
- bias_main: float32 [4, 4096], P('section'), may hold values from -1 to 1
- bias_down: float32 [2, 2, 1024], replicated, may hold values from -1 to 1
- cotangent: bfloat16 [2, 8, 512, 1024], P(None, 'dp'), may hold values from -6 to 6
Outputs:
- hidden_states: bfloat16 [4, 2, 8, 512, 1024], P('section', None, 'dp')
- input_grads: bfloat16 [4, 2, 8, 512, 1024], P('section', None, 'dp')
- grad_bias_main: float32 [4, 4096], replicated
- grad_bias_down: float32 [2, 2, 1024], replicated
The draws below stay inside these ranges and needn't reach their ends.
Inputs may be any that keep to these rules, and one draw needn't show every extreme that they name: `lengths`: some sequence in every draw has all 512 tokens valid.
All inputs are finite; a program needn't handle non-finite values.
Results may differ from the reference program's by a relative error of at most 0.015.
Values may be sent and summed in bfloat16 or wider, within the bound.
No kernel may reach another device: no remote copies, remote signals or barrier semaphores. Data moves between devices by JAX's collectives and lax.ppermute only.
A program may use at most 192 MiB of HBM per device.

```python
import math
import jax
import jax.numpy as jnp
from jax import lax

D = 1024
HEADS = 16
HEAD = 64
FF = 4096
LEN = 512
MB = 2
SEQS = 8
N_SECTION = 4


def draw_lengths(key, part):
    key = jax.random.fold_in(key, 11)
    drawn = jax.random.randint(key, (MB * SEQS,), LEN // 4, LEN + 1)
    chosen = jax.random.randint(jax.random.fold_in(key, 1), (), 0, MB * SEQS)
    drawn = jnp.where(jnp.arange(MB * SEQS) == chosen, LEN, drawn)
    return drawn.reshape(MB, SEQS).astype(jnp.int32)


def draw_w_main(key, part):
    key = jax.random.fold_in(key, 5)
    normal_part = jax.random.normal(key, (N_SECTION, D, FF), jnp.float32)
    section_ids = jnp.arange(N_SECTION)[:, None, None]
    columns = jnp.arange(FF)[None, None, :]
    boost = jnp.where((section_ids % 2 == 0) & (columns >= 3 * D), math.sqrt(LEN / 4), 1.0)
    return (normal_part * boost * D ** (-0.5)).astype(jnp.bfloat16)


def block_levels(rng, extent, cuts, least, top_value):
    factor_of = 1.0
    for dim, blocks in cuts:
        draws = jax.random.uniform(jax.random.fold_in(jax.random.fold_in(rng, 6), dim), (blocks,), jnp.float32, least / len(cuts), top_value / len(cuts))
        factor_of = factor_of * jnp.repeat(jnp.exp(draws), extent[dim] // blocks).reshape((-1,) + (1,) * (len(extent) - 1 - dim))
    return factor_of


def gaussian(own_key, shape, width, limit, shards=(), kind=jnp.bfloat16):
    values = jax.random.normal(own_key, shape, jnp.float32) * width
    if len(shards) > 0:
        values = block_levels(own_key, shape, shards, -0.22, 0.18) * values
    return jnp.clip(values, min=-limit, max=limit).astype(kind)


def setup_inputs(seed: int = 0) -> dict:
    key_list = jax.random.split(jax.random.key(seed), 9)
    inputs_x = gaussian(key_list[0], (MB, SEQS, LEN, D), 1.0, 6.0, ((1, 8),))
    lengths = draw_lengths(jax.random.fold_in(key_list[8], 71), 0)
    w_main = draw_w_main(jax.random.fold_in(key_list[8], 71), 0)
    w_down = gaussian(key_list[3], (2, FF, D), FF ** -0.5, 0.09375)
    gains = jnp.clip(1.0 + 0.1 * jax.random.normal(key_list[4], (N_SECTION, D), jnp.float32), 0.5, 1.5)
    bias_main = gaussian(key_list[5], (N_SECTION, FF), 0.2, 1.0, ((0, 4),), jnp.float32)
    bias_down = gaussian(key_list[6], (2, 2, D), 0.2, 1.0, (), jnp.float32)
    cotangent = gaussian(key_list[7], (MB, SEQS, LEN, D), 1.0, 6.0, ((1, 8),))
    return {"inputs_x": inputs_x, "lengths": lengths, "w_main": w_main, "w_down": w_down, "gains": gains, "bias_main": bias_main, "bias_down": bias_down, "cotangent": cotangent}


@jax.custom_vjp
def low(v):
    return lax.optimization_barrier(v.astype(jnp.bfloat16)).astype(jnp.float32)

@jax.custom_vjp
def low_back(v):
    return v

def low_keep(v):
    return (low(v), None)

def low_pass(kept, grad):
    return (grad,)

def back_keep(v):
    return (v, None)

def back_low(kept, grad):
    return (low(grad),)
low.defvjp(low_keep, low_pass)
low_back.defvjp(back_keep, back_low)
EPSILON = 1e-12
NEGATIVE = -1e+30
HIGHEST = lax.Precision.HIGHEST

def layer_norm(residual, norm_gain, norm_shift):
    center = residual - lax.optimization_barrier(jnp.mean(residual, axis=-1, keepdims=True))
    spread = lax.optimization_barrier(jnp.mean(center * center, axis=-1, keepdims=True))
    return center * lax.rsqrt(spread + EPSILON) * norm_gain + norm_shift

def attention_section(hidden, weight, biases, norm_gain, key_valid):
    group_size = hidden.shape[0]
    row_count = hidden.shape[1]
    projected = low_back(jnp.einsum('gtd,de->gte', hidden, weight[:, :3 * D], precision=HIGHEST))
    queries = low(projected[..., :D] + biases[:D]).reshape(group_size, row_count, HEADS, HEAD)
    keys_low = low(projected[..., D:2 * D]).reshape(group_size, row_count, HEADS, HEAD)
    values_low = low(projected[..., 2 * D:] + biases[D:2 * D]).reshape(group_size, row_count, HEADS, HEAD)
    raw_scores = jnp.einsum('gqhd,gkhd->ghqk', queries, keys_low, precision=HIGHEST) * HEAD ** (-0.5)
    scores = low_back(jnp.where(key_valid[:, None, None, :], raw_scores, NEGATIVE))
    row_top = lax.optimization_barrier(jnp.max(scores, axis=-1, keepdims=True))
    log_total = row_top + jnp.log(lax.optimization_barrier(jnp.sum(jnp.exp(scores - row_top), axis=-1, keepdims=True)))
    probabilities = low(jnp.exp(scores - log_total))
    attended = jnp.einsum('ghqk,gkhd->gqhd', probabilities, values_low, precision=HIGHEST)
    attended = low(low_back(attended.reshape(group_size, row_count, D)))
    output_part = low_back(jnp.einsum('gtd,de->gte', attended, weight[:, 3 * D:], precision=HIGHEST))
    residual = hidden + output_part + biases[2 * D:3 * D]
    return low_back(low(layer_norm(residual, norm_gain, biases[3 * D:])))

def feed_forward_section(hidden, w_first, w_second, first_bias, down_pair, norm_gain):
    projected = low_back(jnp.einsum('gtd,de->gte', hidden, w_first, precision=HIGHEST)) + first_bias
    activated = low(jax.nn.gelu(projected, approximate=False))
    second_part = low_back(jnp.einsum('gte,ed->gtd', activated, w_second, precision=HIGHEST))
    residual = hidden + second_part + down_pair[0]
    return low_back(low(layer_norm(residual, norm_gain, down_pair[1])))

def reference(inputs_x, lengths, w_main, w_down, gains, bias_main, bias_down, cotangent):
    total_seqs = MB * SEQS
    group_size = math.gcd(4, total_seqs)
    group_count = total_seqs // group_size
    main_weights = w_main.astype(jnp.float32)
    down_weights = w_down.astype(jnp.float32)
    inputs_all = inputs_x.astype(jnp.float32).reshape(group_count, group_size, LEN, D)
    grads_all = cotangent.astype(jnp.float32).reshape(group_count, group_size, LEN, D)
    lengths_all = lengths.reshape(group_count, group_size)
    positions = jnp.arange(LEN, dtype=jnp.int32)

    def one_group(carried, pieces):
        main_totals, down_totals = carried
        current, lengths_now, gradient = pieces
        key_valid = positions[None, :] < lengths_now[:, None]
        pullbacks = []
        section_outputs = []
        for section_index in range(N_SECTION):
            layer_index = section_index // 2
            if section_index % 2 == 0:

                def attention_part(hidden, biases, section_index=section_index):
                    return attention_section(hidden, main_weights[section_index], biases, gains[section_index], key_valid)
                current, pullback = jax.vjp(attention_part, current, bias_main[section_index])
            else:

                def feed_forward(hidden, biases, down_pair, section_index=section_index, layer_index=layer_index):
                    return feed_forward_section(hidden, main_weights[section_index], down_weights[layer_index], biases, down_pair, gains[section_index])
                current, pullback = jax.vjp(feed_forward, current, bias_main[section_index], bias_down[layer_index])
            pullbacks.append(pullback)
            section_outputs.append(current)
        section_grads = [None] * N_SECTION
        main_rows = [None] * N_SECTION
        down_terms = jnp.zeros((2, 2, D), jnp.float32)
        for section_index in reversed(range(N_SECTION)):
            pulled = pullbacks[section_index](gradient)
            gradient = pulled[0]
            section_grads[section_index] = gradient
            main_rows[section_index] = pulled[1]
            if section_index % 2 == 1:
                down_terms = down_terms.at[section_index // 2].add(pulled[2])
        main_totals = main_totals + jnp.stack(main_rows)
        down_totals = down_totals + down_terms
        return ((main_totals, down_totals), (jnp.stack(section_outputs).astype(jnp.bfloat16), jnp.stack(section_grads).astype(jnp.bfloat16)))
    start = (jnp.zeros((N_SECTION, FF), jnp.float32), jnp.zeros((2, 2, D), jnp.float32))
    totals, stacked = lax.scan(one_group, start, (inputs_all, lengths_all, grads_all))
    hidden_all = jnp.moveaxis(stacked[0], 1, 0).reshape(N_SECTION, MB, SEQS, LEN, D)
    grads_out = jnp.moveaxis(stacked[1], 1, 0).reshape(N_SECTION, MB, SEQS, LEN, D)
    return (hidden_all, grads_out, totals[0], totals[1])
```

```python
import functools

import jax
import jax.numpy as jnp
from jax import lax
from jax.experimental import pallas as pl
from jax.experimental.pallas import tpu as pltpu
from jax.sharding import PartitionSpec as P

D = 1024
HEADS = 16
HEAD = 64
FF = 4096
EPSILON = 1e-12
NEGATIVE = -1e30
CHUNKS = 4

F32, BF16 = (jnp.float32, jnp.bfloat16)
NN = (((1,), (0,)), ((), ()))
NT = (((1,), (1,)), ((), ()))
TN = (((0,), (0,)), ((), ()))
IN_VMEM = pl.BlockSpec(memory_space=pltpu.VMEM)
IN_SMEM = pl.BlockSpec(memory_space=pltpu.SMEM)
IN_HBM = pl.BlockSpec(memory_space=pl.ANY)
SHAPE = jax.ShapeDtypeStruct


def dot(left, right, dims=NN):
    return lax.dot_general(left, right, dims, preferred_element_type=F32)


def fetch_main(place, row, sources, blocks, kept, sems):
    own, received = (sources[0], sources[1:])
    rows = D // CHUNKS
    for slot, block in blocks:

        @pl.when(place[row, block] == 0)
        def _():
            pltpu.make_async_copy(
                own.at[:, pl.ds(block * D, D)], kept.at[slot], sems.at[slot]
            ).start()

        for which in range(len(received) // CHUNKS):

            @pl.when(place[row, block] == 1 + which)
            def _():
                for chunk in range(CHUNKS):
                    pltpu.make_async_copy(
                        received[which * CHUNKS + chunk],
                        kept.at[slot, pl.ds(chunk * rows, rows), :],
                        sems.at[slot],
                    ).start()


def fetch_down(w_down, layer, block, kept, slot, sems):
    pltpu.make_async_copy(
        w_down.at[layer, pl.ds(block * D, D), :], kept.at[slot], sems.at[slot]
    ).start()


def wait_slot(w_down, kept, slot, sems):
    pltpu.make_async_copy(w_down.at[0, pl.ds(0, D), :], kept.at[slot], sems.at[slot]).wait()


def norm_forward(residual, gain, shift):
    center = residual - jnp.mean(residual, axis=1, keepdims=True)
    scale = lax.rsqrt(jnp.mean(center * center, axis=1, keepdims=True) + EPSILON)
    normed = center * scale
    return ((normed * gain + shift).astype(BF16), normed.astype(BF16), scale)


def norm_backward(grad, normed, scale, gain):
    up = grad * gain
    first = jnp.mean(up, axis=1, keepdims=True)
    second = jnp.mean(up * normed, axis=1, keepdims=True)
    return (up - first - normed * second) * scale


def lane_halves():
    lane = lax.broadcasted_iota(jnp.int32, (1, 128), 1)
    return (lane < HEAD, lane >= HEAD)


def project(hidden, biases, kept, slots, q_out, kv_out, wait):
    wait(slots[0])
    queries = (dot(hidden, kept[slots[0]]) + biases[:, :D]).astype(BF16)
    q_out[...] = queries * BF16(HEAD ** (-0.5))
    wait(slots[1])
    kv_out[:, :D] = dot(hidden, kept[slots[1]]).astype(BF16)
    wait(slots[2])
    kv_out[:, D:] = (dot(hidden, kept[slots[2]]) + biases[:, D : 2 * D]).astype(BF16)


def attend(q_ref, kv, length, attended, log_out):
    rows, keys = (q_ref.shape[0], kv.shape[0])
    position = lax.broadcasted_iota(jnp.int32, (1, keys), 1)
    mask = jnp.where(position < length, 0.0, NEGATIVE).astype(F32)
    halves = lane_halves()
    lane = lax.broadcasted_iota(jnp.int32, (1, 128), 1)
    tops = jnp.zeros((rows, 128), F32)
    sums = jnp.ones((rows, 128), F32)
    for pair in range(HEADS // 2):
        at = slice(pair * 128, pair * 128 + 128)
        keys_pair, values_pair, queries = (kv[:, at], kv[:, D + at.start : D + at.stop], q_ref[:, at])
        parts = []
        for which in range(2):
            mine = halves[which]
            scores = dot(jnp.where(mine, queries, BF16(0)), keys_pair, NT) + mask
            top = jnp.max(scores, axis=1, keepdims=True)
            powers = jnp.exp(scores - top).astype(BF16)
            both = dot(powers, jnp.where(mine, values_pair, BF16(1)))
            parts.append(both * (1.0 / pltpu.roll(both, HEAD, 1)))
            place = lane == (HEAD * (1 - which) + pair)
            tops = jnp.where(place, top, tops)
            sums = jnp.where(place, both, sums)
        attended[:, at] = jnp.where(halves[0], parts[0], parts[1]).astype(BF16)
    log_out[...] = (tops + jnp.log(sums)).T


def attend_backward(grad_att, q_ref, kv, log_ref, mask, dq_out, dkv):
    halves = lane_halves()
    for pair in range(HEADS // 2):
        at = slice(pair * 128, pair * 128 + 128)
        low = slice(D + at.start, D + at.stop)
        keys_pair, values_pair, queries, grads = (kv[:, at], kv[:, low], q_ref[:, at], grad_att[:, at])
        grad_q = grad_k = grad_v = None
        for which in range(2):
            mine = halves[which]
            q_mine = jnp.where(mine, queries, BF16(0))
            g_mine = jnp.where(mine, grads, BF16(0))
            row = HEAD * (1 - which) + pair
            scores = dot(keys_pair, q_mine, NT) + mask[...]
            soft = jnp.exp(scores - log_ref[row : row + 1, :])
            grad_soft = dot(values_pair, g_mine, NT)
            total = jnp.sum(soft * grad_soft, axis=0, keepdims=True)
            grad_scores = (soft * (grad_soft - total)).astype(BF16)
            part_v = dot(soft.astype(BF16), g_mine)
            part_k = dot(grad_scores, q_mine)
            part_q = dot(grad_scores, jnp.where(mine, keys_pair, BF16(0)), TN)
            grad_v = part_v if which == 0 else grad_v + part_v
            grad_k = part_k if which == 0 else grad_k + part_k
            grad_q = part_q if which == 0 else grad_q + part_q
        dq_out[:, at] = grad_q * HEAD ** (-0.5)
        dkv[:, at] = grad_k
        dkv[:, low] = grad_v


def gelu_pair(value):
    below = 0.5 + 0.5 * lax.erf(value * 0.7071067811865476)
    return (value * below, below + value * (0.3989422804014327 * jnp.exp(value * value * -0.5)))


def feed_forward(hidden, biases, first_slots, second_slots, kept, act, slope, wait):
    total = None
    for block in range(4):
        wait(first_slots[block])
        full = slice(block * D, block * D + D)
        value, grad = gelu_pair(dot(hidden, kept[first_slots[block]]) + biases[:, full])
        slope[:, full] = grad.astype(BF16)
        act[:, full] = value.astype(BF16)
        wait(second_slots[block])
        part = dot(act[:, full], kept[second_slots[block]])
        total = part if total is None else total + part
    return total


def feed_backward(grad_low, slope, first_slots, second_slots, kept, act, bias_out, wait):
    total = None
    for block in range(4):
        full = slice(block * D, block * D + D)
        wait(second_slots[block])
        grad = dot(grad_low, kept[second_slots[block]], NT) * slope[:, full].astype(F32)
        bias_out[:, full] = jnp.sum(grad, axis=0, keepdims=True)
        act[:, full] = grad.astype(BF16)
        wait(first_slots[block])
        part = dot(act[:, full], kept[first_slots[block]], NT)
        total = part if total is None else total + part
    return total


def gather_keys(kv_own, kv_other, half, kv, sems):
    rows = kv_own.shape[0]
    mine = pltpu.make_async_copy(kv_own, kv.at[pl.ds(pl.multiple_of(half * rows, rows), rows), :], sems.at[0])
    other = pltpu.make_async_copy(
        kv_other, kv.at[pl.ds(pl.multiple_of((1 - half) * rows, rows), rows), :], sems.at[1]
    )
    return (mine, other)


def first_kernel(n_main, place, hidden, main_bias, w_down, *refs):
    sources = refs[:n_main]
    q_out, kv_out, kept, sems = refs[n_main:]
    fetch_main(place, 0, sources, ((0, 0), (1, 1), (2, 2)), kept, sems)
    wait = lambda slot: wait_slot(w_down, kept, slot, sems)
    project(hidden[...], main_bias[0:1, :], kept, (0, 1, 2), q_out, kv_out, wait)


def low_kernel(n_main, place, info, hidden, q_in, main_bias, down_bias, gains, kv_own, kv_other, w_down, *refs):
    sources = refs[:n_main]
    (
        mid_out, out_out, q_out, kv_out, log_out, norm_a, scale_a, norm_f, scale_f, slope,
        kept, sems, kv, kv_sems, attended, act,
    ) = refs[n_main:]
    loads = gather_keys(kv_own, kv_other, info[1], kv, kv_sems)
    for load in loads:
        load.start()
    fetch_main(place, 0, sources, ((0, 3),), kept, sems)
    for block in range(4):
        fetch_main(place, 1, sources, ((1 + block, block),), kept, sems)
        fetch_down(w_down, 0, block, kept, 5 + block, sems)
    fetch_main(place, 2, sources, ((9, 0), (10, 1), (11, 2)), kept, sems)
    wait = lambda slot: wait_slot(w_down, kept, slot, sems)
    for load in loads:
        load.wait()
    attend(q_in, kv, info[0], attended, log_out)
    wait(0)
    residual = hidden[...].astype(F32) + dot(attended[...], kept[0]) + main_bias[0:1, 2 * D : 3 * D]
    mid, norm, scale = norm_forward(residual, gains[0:1, :], main_bias[0:1, 3 * D :])
    mid_out[...] = mid
    norm_a[...] = norm
    scale_a[...] = jnp.broadcast_to(scale, scale_a.shape)
    hidden_now = mid_out[...]
    total = feed_forward(
        hidden_now, main_bias[1:2, :], (1, 2, 3, 4), (5, 6, 7, 8), kept, act, slope, wait
    )
    residual = mid_out[...].astype(F32) + total + down_bias[0:1, :]
    out, norm, scale = norm_forward(residual, gains[1:2, :], down_bias[1:2, :])
    out_out[...] = out
    norm_f[...] = norm
    scale_f[...] = jnp.broadcast_to(scale, scale_f.shape)
    project(out_out[...], main_bias[2:3, :], kept, (9, 10, 11), q_out, kv_out, wait)


def start_attention_backward(grad, norm, scale, gain, w_out, grad_res, grad_att, sums):
    grad_float = grad.astype(F32)
    grad_now = norm_backward(grad_float, norm.astype(F32), scale, gain)
    grad_res[...] = grad_now
    sums[1:2, :] = jnp.sum(grad_now, axis=0, keepdims=True)
    sums[2:3, :] = jnp.sum(grad_float, axis=0, keepdims=True)
    grad_att[...] = dot(grad_now.astype(BF16), w_out, NT).astype(BF16)


def finish_attention_backward(half, dq, dkv, dq_out, own_out, other_out, sums, bv_out):
    rows = dq.shape[0]
    grad_q = dq[...]
    dq_out[...] = grad_q.astype(BF16)
    sums[0:1, :] = jnp.sum(grad_q, axis=0, keepdims=True)
    bv_out[...] = jnp.sum(dkv[:, D:], axis=0, keepdims=True)
    own_out[...] = dkv[pl.ds(pl.multiple_of(half * rows, rows), rows), :]
    other_out[...] = dkv[pl.ds(pl.multiple_of((1 - half) * rows, rows), rows), :].astype(BF16)


def fill_mask(mask, length):
    position = lax.broadcasted_iota(jnp.int32, mask.shape, 0)
    mask[...] = jnp.where(position < length, 0.0, NEGATIVE).astype(F32)


def high_kernel(n_main, place, info, hidden, q_in, cotangent, main_bias, down_bias, gains, kv_own, kv_other, w_down, *refs):
    sources = refs[:n_main]
    (
        mid_out, out_out, ig_out, dq_out, own_out, other_out, grad_res, bias_ff, bias_down, sums, bv_out,
        kept, sems, kv, kv_sems, attended, act, slope, mask, logs, norm_a, dq, dkv,
    ) = refs[n_main:]
    loads = gather_keys(kv_own, kv_other, info[1], kv, kv_sems)
    for load in loads:
        load.start()
    fetch_main(place, 2, sources, ((0, 3),), kept, sems)
    for block in range(4):
        fetch_main(place, 3, sources, ((1 + block, block),), kept, sems)
        fetch_down(w_down, 1, block, kept, 5 + block, sems)
    wait = lambda slot: wait_slot(w_down, kept, slot, sems)
    done = lambda slot: None
    fill_mask(mask, info[0])
    for load in loads:
        load.wait()
    attend(q_in, kv, info[0], attended, logs)
    wait(0)
    residual = hidden[...].astype(F32) + dot(attended[...], kept[0]) + main_bias[2:3, 2 * D : 3 * D]
    mid, norm, scale_mid = norm_forward(residual, gains[2:3, :], main_bias[2:3, 3 * D :])
    mid_out[...] = mid
    norm_a[...] = norm
    hidden_now = mid_out[...]
    total = feed_forward(
        hidden_now, main_bias[3:4, :], (1, 2, 3, 4), (5, 6, 7, 8), kept, act, slope, wait
    )
    residual = mid_out[...].astype(F32) + total + down_bias[2:3, :]
    out, norm, scale = norm_forward(residual, gains[3:4, :], down_bias[3:4, :])
    out_out[...] = out
    grad_float = cotangent[...].astype(F32)
    grad_now = norm_backward(grad_float, norm.astype(F32), scale, gains[3:4, :])
    bias_down[0:1, :] = jnp.sum(grad_now, axis=0, keepdims=True)
    bias_down[1:2, :] = jnp.sum(grad_float, axis=0, keepdims=True)
    total = feed_backward(
        grad_now.astype(BF16), slope, (1, 2, 3, 4), (5, 6, 7, 8), kept, act, bias_ff, done
    )
    ig_out[...] = (grad_now + total).astype(BF16)
    start_attention_backward(
        ig_out[...], norm_a[...], scale_mid, gains[2:3, :], kept[0], grad_res, attended, sums
    )
    attend_backward(attended, q_in, kv, logs, mask, dq, dkv)
    finish_attention_backward(info[1], dq, dkv, dq_out, own_out, other_out, sums, bv_out)


def input_grad(grad_res, dq_in, own_in, recv_in, kept, slots, wait):
    wait(slots[0])
    total = grad_res[...] + dot(dq_in[...], kept[slots[0]], NT)
    grads = (own_in[...] + recv_in[...].astype(F32)).astype(BF16)
    wait(slots[1])
    total = total + dot(grads[:, :D], kept[slots[1]], NT)
    wait(slots[2])
    return (total + dot(grads[:, D:], kept[slots[2]], NT)).astype(BF16)


def back_kernel(
    n_main, place, info, grad_in, dq_in, own_in, recv_in, gains, norm_f, scale_f, slope, norm_a, scale_a, logs, q_in,
    kv_own, kv_other, w_down, *refs
):
    sources = refs[:n_main]
    (
        ig_high, ig_out, dq_out, own_out, other_out, grad_res, bias_ff, bias_down, sums, bv_out,
        kept, sems, kv, kv_sems, grad_att, act, mask, dq, dkv,
    ) = refs[n_main:]
    fetch_main(place, 2, sources, ((9, 0), (10, 1), (11, 2)), kept, sems)
    for block in range(4):
        fetch_down(w_down, 0, block, kept, 5 + block, sems)
        fetch_main(place, 1, sources, ((1 + block, block),), kept, sems)
    fetch_main(place, 0, sources, ((0, 3),), kept, sems)
    loads = gather_keys(kv_own, kv_other, info[1], kv, kv_sems)
    for load in loads:
        load.start()
    wait = lambda slot: wait_slot(w_down, kept, slot, sems)
    fill_mask(mask, info[0])
    ig_high[...] = input_grad(grad_in, dq_in, own_in, recv_in, kept, (9, 10, 11), wait)
    grad_float = ig_high[...].astype(F32)
    grad_now = norm_backward(grad_float, norm_f[...].astype(F32), scale_f[:, 0:1], gains[1:2, :])
    bias_down[0:1, :] = jnp.sum(grad_now, axis=0, keepdims=True)
    bias_down[1:2, :] = jnp.sum(grad_float, axis=0, keepdims=True)
    total = feed_backward(
        grad_now.astype(BF16), slope, (1, 2, 3, 4), (5, 6, 7, 8), kept, act, bias_ff, wait
    )
    ig_out[...] = (grad_now + total).astype(BF16)
    wait(0)
    start_attention_backward(
        ig_out[...], norm_a[...], scale_a[:, 0:1], gains[0:1, :], kept[0], grad_res, grad_att, sums
    )
    for load in loads:
        load.wait()
    attend_backward(grad_att, q_in, kv, logs, mask, dq, dkv)
    finish_attention_backward(info[1], dq, dkv, dq_out, own_out, other_out, sums, bv_out)


def last_kernel(n_main, place, grad_res, dq_in, own_in, recv_in, w_down, *refs):
    sources = refs[:n_main]
    ig_out, kept, sems = refs[n_main:]
    fetch_main(place, 0, sources, ((0, 0), (1, 1), (2, 2)), kept, sems)
    wait = lambda slot: wait_slot(w_down, kept, slot, sems)
    ig_out[...] = input_grad(grad_res, dq_in, own_in, recv_in, kept, (0, 1, 2), wait)


def launch(kernel, name, outs, scratch, smem, vmem, hbm):
    return pl.pallas_call(
        functools.partial(kernel, len(hbm[1])),
        name=name,
        out_shape=outs,
        in_specs=[IN_SMEM] * len(smem)
        + [IN_VMEM] * len(vmem)
        + [IN_HBM] * (len(hbm[0]) + len(hbm[1])),
        out_specs=[IN_VMEM] * len(outs),
        scratch_shapes=scratch,
        compiler_params=pltpu.CompilerParams(vmem_limit_bytes=58 * 2**20),
    )(*smem, *vmem, *hbm[0], *hbm[1])


def main_slots(count):
    return [pltpu.VMEM((count, D, D), BF16), pltpu.SemaphoreType.DMA((count,))]


def flip(value, axis, bit):
    count = lax.axis_size(axis)
    return lax.ppermute(value, axis, [(source, source ^ bit) for source in range(count)])


def gather_weights(own, base):
    block = lax.dynamic_slice_in_dim(own, base * D, D, axis=1)
    rows = D // CHUNKS
    pieces = [block[i * rows : i * rows + rows] for i in range(CHUNKS)]
    x_near = [flip(piece, "section", 1) for piece in pieces]
    y_near = [flip(piece, "section", 2) for piece in pieces]
    x_far = [flip(piece, "dp", 2) for piece in x_near]
    y_far = [flip(piece, "dp", 2) for piece in y_near]
    d_near = [flip(piece, "section", 1) for piece in y_near]
    d_far = [flip(piece, "section", 2) for piece in x_far]
    gathered = []
    for near, far in ((x_near, x_far), (y_near, y_far), (d_near, d_far)):
        near_core = [flip(piece, "dp", 1) for piece in near]
        far_core = [flip(piece, "dp", 1) for piece in far]
        gathered += [near, far, near_core, far_core]
    return [piece for group in gathered for piece in group]


def butterfly(value):
    for axis in ("dp", "section"):
        bit = 1
        while bit < lax.axis_size(axis):
            value = value + flip(value, axis, bit)
            bit *= 2
    return value


def pick(stack, index):
    return lax.dynamic_index_in_dim(stack, index, 0, keepdims=False)


def spread(mine, got_x, got_y, got_d, section, core):
    same = core == section % 2
    keep_first = jnp.where(same, mine, got_x)
    keep_second = jnp.where(same, got_y, got_d)
    send = jnp.stack([jnp.where(same, got_x, mine), jnp.where(same, got_d, got_y)])
    got = flip(send, "dp", 1)
    batch = section // 2
    kept_rows = [jnp.where(batch == 0, keep_first, keep_second), jnp.where(batch == 0, keep_second, keep_first)]
    got_rows = [jnp.where(batch == 0, got[0], got[1]), jnp.where(batch == 0, got[1], got[0])]
    parts = []
    for kept_now, got_now in zip(kept_rows, got_rows):
        parts.append(
            jnp.concatenate(
                [jnp.where(core == 0, kept_now, got_now), jnp.where(core == 0, got_now, kept_now)]
            )
        )
    return jnp.stack(parts)[None, :, None]


def per_device(inputs_x, lengths, w_main, w_down, gains, bias_main, bias_down, cotangent):
    section = lax.axis_index("section")
    lane = lax.axis_index("dp")
    core, plane = (lane % 2, (lane // 2) % 2)
    base = core * 2 + plane
    rows = inputs_x.shape[2] // 2

    batch = section // 2
    same = core == section % 2
    whole = jnp.stack([pick(inputs_x[:, 0], batch), pick(cotangent[:, 0], batch)])
    mine = lax.dynamic_slice_in_dim(whole, core * rows, rows, axis=1)
    other = flip(lax.dynamic_slice_in_dim(whole, (1 - core) * rows, rows, axis=1), "dp", 1)
    mine = jnp.where(same, mine, other)
    hidden, grad_last = (mine[0], mine[1])
    length_own = lax.dynamic_slice_in_dim(lengths[:, 0], batch, 1).astype(F32)
    length_other = flip(jnp.broadcast_to(length_own[None], (8, 128)), "dp", 1)[0, :1]
    length = jnp.where(same, length_own, length_other).astype(jnp.int32)
    info = jnp.concatenate([length, core[None].astype(jnp.int32)])

    small = jnp.concatenate([gains, bias_main], axis=1)
    smalls = jnp.stack([small, flip(small, "section", 1), flip(small, "section", 2), flip(small, "section", 3)])
    smalls = jnp.concatenate([pick(smalls, section ^ s) for s in range(4)])
    all_gains, all_bias = (smalls[:, :D], smalls[:, D:])
    down_bias = bias_down.reshape(4, D)

    own = w_main[0]
    received = gather_weights(own, base)
    blocks = jnp.arange(4, dtype=jnp.int32)[None, :]
    away = section ^ jnp.arange(4, dtype=jnp.int32)[:, None]
    place = jnp.where(away == 0, 0, 1 + (away - 1) * 4 + (blocks ^ base)).astype(jnp.int32)
    sources = [own] + received

    def row(width, kind):
        return SHAPE((rows, width), kind)

    pair_sems = pltpu.SemaphoreType.DMA((2,))
    keys = pltpu.VMEM((2 * rows, 2 * D), BF16)
    q0, kv0 = launch(
        first_kernel, "first", [row(D, BF16), row(2 * D, BF16)], main_slots(3),
        [place], [hidden, all_bias], ([w_down], sources),
    )
    kv0_other = flip(kv0, "dp", 1)
    hs0, hs1, q2, kv2, logs0, norm0, scale0, norm1, scale1, slope1 = launch(
        low_kernel, "low",
        [
            row(D, BF16), row(D, BF16), row(D, BF16), row(2 * D, BF16), SHAPE((128, rows), F32),
            row(D, BF16), row(128, F32), row(D, BF16), row(128, F32), row(FF, BF16),
        ],
        main_slots(12)
        + [keys, pair_sems, pltpu.VMEM((rows, D), BF16), pltpu.VMEM((rows, FF), BF16)],
        [place, info], [hidden, q0, all_bias, down_bias, all_gains], ([kv0, kv0_other, w_down], sources),
    )
    kv2_other = flip(kv2, "dp", 1)
    hs2, hs3, ig3, dq2, own2, other2, res2, bias3, pair3, sums2, bv2 = launch(
        high_kernel, "high",
        [
            row(D, BF16), row(D, BF16), row(D, BF16), row(D, BF16), row(2 * D, F32), row(2 * D, BF16),
            row(D, F32), SHAPE((1, FF), F32), SHAPE((2, D), F32), SHAPE((3, D), F32), SHAPE((1, D), F32),
        ],
        main_slots(9)
        + [
            keys, pair_sems, pltpu.VMEM((rows, D), BF16), pltpu.VMEM((rows, FF), BF16),
            pltpu.VMEM((rows, FF), BF16), pltpu.VMEM((2 * rows, rows), F32), pltpu.VMEM((128, rows), F32),
            pltpu.VMEM((rows, D), BF16), pltpu.VMEM((rows, D), F32), pltpu.VMEM((2 * rows, 2 * D), F32),
        ],
        [place, info], [hs1, q2, grad_last, all_bias, down_bias, all_gains],
        ([kv2, kv2_other, w_down], sources),
    )
    recv2 = flip(other2, "dp", 1)
    ig2, ig1, dq0, own0, other0, res0, bias1, pair1, sums0, bv0 = launch(
        back_kernel, "back",
        [
            row(D, BF16), row(D, BF16), row(D, BF16), row(2 * D, F32), row(2 * D, BF16), row(D, F32),
            SHAPE((1, FF), F32), SHAPE((2, D), F32), SHAPE((3, D), F32), SHAPE((1, D), F32),
        ],
        main_slots(12)
        + [
            keys, pair_sems, pltpu.VMEM((rows, D), BF16), pltpu.VMEM((rows, FF), BF16),
            pltpu.VMEM((2 * rows, rows), F32), pltpu.VMEM((rows, D), F32), pltpu.VMEM((2 * rows, 2 * D), F32),
        ],
        [place, info],
        [res2, dq2, own2, recv2, all_gains, norm1, scale1, slope1, norm0, scale0, logs0, q0],
        ([kv0, kv0_other, w_down], sources),
    )
    recv0 = flip(other0, "dp", 1)
    (ig0,) = launch(
        last_kernel, "last", [row(D, BF16)], main_slots(3), [place], [res0, dq0, own0, recv0], ([w_down], sources)
    )

    outputs = jnp.stack([hs0, hs1, hs2, hs3])
    hidden_states = spread(
        pick(outputs, section),
        *(flip(pick(outputs, section ^ bits), "section", bits) for bits in (1, 2, 3)),
        section, core,
    )
    grads = jnp.stack([ig0, ig1, ig2, ig3])
    moved = []
    for bits in (1, 2, 3):
        early = [(s, s ^ bits) for s in range(4) if s ^ bits != 0]
        got = lax.ppermute(pick(jnp.stack([ig1, ig1, ig2, ig3]), section ^ bits), "section", early)
        last = lax.ppermute(ig0, "section", [(bits, 0)])
        moved.append(jnp.where(section == 0, last, got))
    input_grads = spread(pick(grads, section), *moved, section, core)

    def attention_terms(sums, bv):
        return jnp.concatenate([sums[0:1], bv, sums[1:2], sums[2:3]], axis=1)

    terms = jnp.concatenate(
        [attention_terms(sums0, bv0), bias1, attention_terms(sums2, bv2), bias3, pair1.reshape(1, -1), pair3.reshape(1, -1)],
        axis=1,
    ).reshape(-1, 128)
    terms = butterfly(terms).reshape(-1)
    main_size = 4 * FF
    return (hidden_states, input_grads, terms[:main_size].reshape(4, FF), terms[main_size:].reshape(2, 2, D))


def solution(mesh):
    placed = (
        P(None, "dp", None, None),
        P(None, "dp"),
        P("section", None, None),
        P(),
        P("section", None),
        P("section", None),
        P(),
        P(None, "dp", None, None),
    )
    return jax.shard_map(
        per_device,
        mesh=mesh,
        in_specs=placed,
        out_specs=(
            P("section", None, "dp", None, None),
            P("section", None, "dp", None, None),
            P(),
            P(),
        ),
        check_vma=False,
    )
```

```python
import functools

import jax
import jax.numpy as jnp
from jax import lax
from jax.experimental import pallas as pl
from jax.experimental.pallas import tpu as pltpu
from jax.sharding import PartitionSpec as P

D = 1024
HEADS = 16
HEAD = 64
FF = 4096
EPSILON = 1e-12
NEGATIVE = -1e30
EXTRA = 16

F32, BF16 = (jnp.float32, jnp.bfloat16)
NN = (((1,), (0,)), ((), ()))
NT = (((1,), (1,)), ((), ()))
TN = (((0,), (0,)), ((), ()))
IN_VMEM = pl.BlockSpec(memory_space=pltpu.VMEM)
IN_SMEM = pl.BlockSpec(memory_space=pltpu.SMEM)
IN_HBM = pl.BlockSpec(memory_space=pl.ANY)
SHAPE = jax.ShapeDtypeStruct


def dot(left, right, dims=NN):
    return lax.dot_general(left, right, dims, preferred_element_type=F32)


HALF, QUARTER = (D // 2, D // 4)
PIECES = (
    ((1, 0, 0, HALF), (2, 0, HALF, HALF)),
    ((3, 0, 0, HALF), (4, 0, HALF, HALF)),
    ((5, 0, 0, HALF), (6, 0, HALF, HALF)),
    ((7, 0, 0, HALF), (8, 0, HALF, HALF)),
    ((9, 0, 0, HALF), (10, 0, HALF, HALF)),
    ((11, 0, 0, HALF + QUARTER), (12, HALF, HALF + QUARTER, QUARTER)),
    ((13, 0, 0, HALF), (14, 0, HALF, HALF)),
    ((15, 0, 0, HALF + QUARTER), (16, HALF, HALF + QUARTER, QUARTER)),
    ((17, 0, 0, HALF), (18, 0, HALF, HALF)),
    ((19, 0, 0, HALF), (12, 0, HALF, HALF)),
    ((20, 0, 0, HALF), (21, 0, HALF, HALF)),
    ((22, 0, 0, HALF), (16, 0, HALF, HALF)),
)


def fetch_main(place, row, sources, blocks, kept, sems):
    for slot, block in blocks:

        @pl.when(place[row, block] == 0)
        def _():
            pltpu.make_async_copy(
                sources[0].at[:, pl.ds(block * D, D)], kept.at[slot], sems.at[slot]
            ).start()

        for which, pieces in enumerate(PIECES):

            @pl.when(place[row, block] == 1 + which)
            def _():
                for source, at, to, rows in pieces:
                    pltpu.make_async_copy(
                        sources[source].at[pl.ds(at, rows), :],
                        kept.at[slot, pl.ds(to, rows), :],
                        sems.at[slot],
                    ).start()


def fetch_down(w_down, layer, block, kept, slot, sems):
    pltpu.make_async_copy(
        w_down.at[layer, pl.ds(block * D, D), :], kept.at[slot], sems.at[slot]
    ).start()


def wait_slot(w_down, kept, slot, sems):
    pltpu.make_async_copy(w_down.at[0, pl.ds(0, D), :], kept.at[slot], sems.at[slot]).wait()


def norm_forward(residual, gain, shift):
    center = residual - jnp.mean(residual, axis=1, keepdims=True)
    scale = lax.rsqrt(jnp.mean(center * center, axis=1, keepdims=True) + EPSILON)
    normed = center * scale
    return ((normed * gain + shift).astype(BF16), normed.astype(BF16), scale)


def norm_backward(grad, normed, scale, gain):
    up = grad * gain
    first = jnp.mean(up, axis=1, keepdims=True)
    second = jnp.mean(up * normed, axis=1, keepdims=True)
    return (up - first - normed * second) * scale


def lane_halves():
    lane = lax.broadcasted_iota(jnp.int32, (1, 128), 1)
    return (lane < HEAD, lane >= HEAD)


def project(hidden, biases, kept, slots, q_out, kv_out, wait):
    wait(slots[0])
    queries = (dot(hidden, kept[slots[0]]) + biases[:, :D]).astype(BF16)
    q_out[...] = queries * BF16(HEAD ** (-0.5))
    wait(slots[1])
    kv_out[:, :D] = dot(hidden, kept[slots[1]]).astype(BF16)
    wait(slots[2])
    kv_out[:, D:] = (dot(hidden, kept[slots[2]]) + biases[:, D : 2 * D]).astype(BF16)


def attend(q_ref, kv, length, attended, log_out, step):
    rows, keys = (q_ref.shape[0], kv.shape[0])
    position = lax.broadcasted_iota(jnp.int32, (1, keys), 1)
    mask = jnp.where(position < length, 0.0, NEGATIVE).astype(F32)
    halves = lane_halves()
    lane = lax.broadcasted_iota(jnp.int32, (1, 128), 1)
    tops = jnp.zeros((rows, 128), F32)
    sums = jnp.ones((rows, 128), F32)
    for pair in range(HEADS // 2):
        step()
        at = slice(pair * 128, pair * 128 + 128)
        keys_pair, values_pair, queries = (kv[:, at], kv[:, D + at.start : D + at.stop], q_ref[:, at])
        parts = []
        for which in range(2):
            mine = halves[which]
            scores = dot(jnp.where(mine, queries, BF16(0)), keys_pair, NT) + mask
            top = jnp.max(scores, axis=1, keepdims=True)
            powers = jnp.exp(scores - top).astype(BF16)
            both = dot(powers, jnp.where(mine, values_pair, BF16(1)))
            parts.append(both * (1.0 / pltpu.roll(both, HEAD, 1)))
            place = lane == (HEAD * (1 - which) + pair)
            tops = jnp.where(place, top, tops)
            sums = jnp.where(place, both, sums)
        attended[:, at] = jnp.where(halves[0], parts[0], parts[1]).astype(BF16)
    log_out[...] = (tops + jnp.log(sums)).T


def attend_backward(grad_att, q_ref, kv, log_ref, mask, dq_out, dkv):
    halves = lane_halves()
    for pair in range(HEADS // 2):
        at = slice(pair * 128, pair * 128 + 128)
        low = slice(D + at.start, D + at.stop)
        keys_pair, values_pair, queries, grads = (kv[:, at], kv[:, low], q_ref[:, at], grad_att[:, at])
        grad_q = grad_k = grad_v = None
        for which in range(2):
            mine = halves[which]
            q_mine = jnp.where(mine, queries, BF16(0))
            g_mine = jnp.where(mine, grads, BF16(0))
            row = HEAD * (1 - which) + pair
            scores = dot(keys_pair, q_mine, NT) + mask[...]
            soft = jnp.exp(scores - log_ref[row : row + 1, :])
            grad_soft = dot(values_pair, g_mine, NT)
            total = jnp.sum(soft * grad_soft, axis=0, keepdims=True)
            grad_scores = (soft * (grad_soft - total)).astype(BF16)
            part_v = dot(soft.astype(BF16), g_mine)
            part_k = dot(grad_scores, q_mine)
            part_q = dot(grad_scores, jnp.where(mine, keys_pair, BF16(0)), TN)
            grad_v = part_v if which == 0 else grad_v + part_v
            grad_k = part_k if which == 0 else grad_k + part_k
            grad_q = part_q if which == 0 else grad_q + part_q
        dq_out[:, at] = grad_q * HEAD ** (-0.5)
        dkv[:, at] = grad_k
        dkv[:, low] = grad_v


def gelu_pair(value):
    below = 0.5 + 0.5 * lax.erf(value * 0.7071067811865476)
    return (value * below, below + value * (0.3989422804014327 * jnp.exp(value * value * -0.5)))


def feed_forward(hidden, biases, first_slots, second_slots, kept, act, slope, wait, step):
    total = None
    for block in range(4):
        step()
        wait(first_slots[block])
        full = slice(block * D, block * D + D)
        value, grad = gelu_pair(dot(hidden, kept[first_slots[block]]) + biases[:, full])
        slope[:, full] = grad.astype(BF16)
        act[:, full] = value.astype(BF16)
        wait(second_slots[block])
        part = dot(act[:, full], kept[second_slots[block]])
        total = part if total is None else total + part
    return total


def feed_backward(grad_low, slope, first_slots, second_slots, kept, act, terms, wait, step):
    total = None
    for block in range(4):
        step()
        full = slice(block * D, block * D + D)
        wait(second_slots[block])
        grad = dot(grad_low, kept[second_slots[block]], NT) * slope[:, full].astype(F32)
        terms[4 + block : 5 + block, :] = jnp.sum(grad, axis=0, keepdims=True)
        act[:, full] = grad.astype(BF16)
        wait(first_slots[block])
        part = dot(act[:, full], kept[first_slots[block]], NT)
        total = part if total is None else total + part
    return total


def gather_keys(kv_own, kv_other, half, kv, sems):
    rows = kv_own.shape[0]
    mine = pltpu.make_async_copy(kv_own, kv.at[pl.ds(pl.multiple_of(half * rows, rows), rows), :], sems.at[0])
    other = pltpu.make_async_copy(
        kv_other, kv.at[pl.ds(pl.multiple_of((1 - half) * rows, rows), rows), :], sems.at[1]
    )
    return (mine, other)


class Loads:
    def __init__(self, place, sources, w_down, kept, sems):
        self.place, self.sources, self.w_down, self.kept, self.sems = (place, sources, w_down, kept, sems)
        self.starts = []

    def main(self, section, *slots):
        for slot, block in slots:
            self.starts.append(
                lambda slot=slot, block=block: fetch_main(
                    self.place, section, self.sources, ((slot, block),), self.kept, self.sems
                )
            )

    def down(self, layer, slot, block):
        self.starts.append(lambda: fetch_down(self.w_down, layer, block, self.kept, slot, self.sems))

    def copies(self, *copies):
        self.starts.append(lambda: [copy.start() for copy in copies])

    def step(self, count=1):
        for _ in range(count):
            if self.starts:
                self.starts.pop(0)()

    def wait(self, slot):
        wait_slot(self.w_down, self.kept, slot, self.sems)


def first_kernel(n_main, place, hidden, main_bias, w_down, *refs):
    sources = refs[:n_main]
    q_out, kv_out, kept, sems = refs[n_main:]
    loads = Loads(place, sources, w_down, kept, sems)
    loads.main(0, (0, 0), (1, 1), (2, 2))
    loads.step(3)
    project(hidden[...], main_bias[0:1, :], kept, (0, 1, 2), q_out, kv_out, loads.wait)


def low_kernel(n_main, place, info, hidden, q_in, main_bias, down_bias, gains, kv_own, kv_other, w_down, *refs):
    sources = refs[:n_main]
    (
        mid_out, out_out, q_out, kv_out, log_out, norm_a, scale_a, norm_f, scale_f, slope,
        kept, sems, kv, kv_sems, attended, act,
    ) = refs[n_main:]
    keys = gather_keys(kv_own, kv_other, info[1], kv, kv_sems)
    loads = Loads(place, sources, w_down, kept, sems)
    wait, step = (loads.wait, loads.step)
    loads.copies(*keys)
    loads.main(0, (0, 3))
    for block in range(4):
        loads.main(1, (1 + block, block))
        loads.down(0, 5 + block, block)
    loads.main(2, (9, 0), (10, 1), (11, 2))
    step(2)
    for key in keys:
        key.wait()
    attend(q_in, kv, info[0], attended, log_out, step)
    wait(0)
    residual = hidden[...].astype(F32) + dot(attended[...], kept[0]) + main_bias[0:1, 2 * D : 3 * D]
    mid, norm, scale = norm_forward(residual, gains[0:1, :], main_bias[0:1, 3 * D :])
    mid_out[...] = mid
    norm_a[...] = norm
    scale_a[...] = jnp.broadcast_to(scale, scale_a.shape)
    hidden_now = mid_out[...]
    total = feed_forward(
        hidden_now, main_bias[1:2, :], (1, 2, 3, 4), (5, 6, 7, 8), kept, act, slope, wait, step
    )
    residual = mid_out[...].astype(F32) + total + down_bias[0:1, :]
    out, norm, scale = norm_forward(residual, gains[1:2, :], down_bias[1:2, :])
    out_out[...] = out
    norm_f[...] = norm
    scale_f[...] = jnp.broadcast_to(scale, scale_f.shape)
    project(out_out[...], main_bias[2:3, :], kept, (9, 10, 11), q_out, kv_out, wait)


def start_attention_backward(grad, norm, scale, gain, w_out, grad_res, grad_att, terms):
    grad_float = grad.astype(F32)
    grad_now = norm_backward(grad_float, norm.astype(F32), scale, gain)
    grad_res[...] = grad_now
    terms[2:3, :] = jnp.sum(grad_now, axis=0, keepdims=True)
    terms[3:4, :] = jnp.sum(grad_float, axis=0, keepdims=True)
    grad_att[...] = dot(grad_now.astype(BF16), w_out, NT).astype(BF16)


def finish_attention_backward(half, dq, dkv, dq_out, own_out, other_out, terms):
    rows = dq.shape[0]
    grad_q = dq[...]
    dq_out[...] = grad_q.astype(BF16)
    terms[0:1, :] = jnp.sum(grad_q, axis=0, keepdims=True)
    terms[1:2, :] = jnp.sum(dkv[:, D:], axis=0, keepdims=True)
    own_out[...] = dkv[pl.ds(pl.multiple_of(half * rows, rows), rows), :].astype(BF16)
    other_out[...] = dkv[pl.ds(pl.multiple_of((1 - half) * rows, rows), rows), :].astype(BF16)


def fill_mask(mask, length):
    position = lax.broadcasted_iota(jnp.int32, mask.shape, 0)
    mask[...] = jnp.where(position < length, 0.0, NEGATIVE).astype(F32)


def high_kernel(n_main, place, info, hidden, q_in, cotangent, main_bias, down_bias, gains, kv_own, kv_other, w_down, *refs):
    sources = refs[:n_main]
    (
        mid_out, out_out, ig_out, dq_out, own_out, other_out, grad_res, terms,
        kept, sems, kv, kv_sems, attended, act, slope, mask, logs, norm_a, dq, dkv,
    ) = refs[n_main:]
    keys = gather_keys(kv_own, kv_other, info[1], kv, kv_sems)
    loads = Loads(place, sources, w_down, kept, sems)
    wait, step = (loads.wait, loads.step)
    loads.copies(*keys)
    loads.main(2, (0, 3))
    for block in range(4):
        loads.main(3, (1 + block, block))
        loads.down(1, 5 + block, block)
    done = lambda slot: None
    step(2)
    fill_mask(mask, info[0])
    for key in keys:
        key.wait()
    attend(q_in, kv, info[0], attended, logs, step)
    wait(0)
    residual = hidden[...].astype(F32) + dot(attended[...], kept[0]) + main_bias[2:3, 2 * D : 3 * D]
    mid, norm, scale_mid = norm_forward(residual, gains[2:3, :], main_bias[2:3, 3 * D :])
    mid_out[...] = mid
    norm_a[...] = norm
    hidden_now = mid_out[...]
    total = feed_forward(
        hidden_now, main_bias[3:4, :], (1, 2, 3, 4), (5, 6, 7, 8), kept, act, slope, wait, step
    )
    residual = mid_out[...].astype(F32) + total + down_bias[2:3, :]
    out, norm, scale = norm_forward(residual, gains[3:4, :], down_bias[3:4, :])
    out_out[...] = out
    grad_float = cotangent[...].astype(F32)
    grad_now = norm_backward(grad_float, norm.astype(F32), scale, gains[3:4, :])
    terms[8:9, :] = jnp.sum(grad_now, axis=0, keepdims=True)
    terms[9:10, :] = jnp.sum(grad_float, axis=0, keepdims=True)
    total = feed_backward(
        grad_now.astype(BF16), slope, (1, 2, 3, 4), (5, 6, 7, 8), kept, act, terms, done, step
    )
    ig_out[...] = (grad_now + total).astype(BF16)
    start_attention_backward(
        ig_out[...], norm_a[...], scale_mid, gains[2:3, :], kept[0], grad_res, attended, terms
    )
    attend_backward(attended, q_in, kv, logs, mask, dq, dkv)
    finish_attention_backward(info[1], dq, dkv, dq_out, own_out, other_out, terms)


def input_grad(grad_res, dq_in, own_in, recv_in, kept, slots, wait, step):
    wait(slots[0])
    step()
    total = grad_res[...] + dot(dq_in[...], kept[slots[0]], NT)
    grads = (own_in[...].astype(F32) + recv_in[...].astype(F32)).astype(BF16)
    wait(slots[1])
    step()
    total = total + dot(grads[:, :D], kept[slots[1]], NT)
    wait(slots[2])
    step()
    return (total + dot(grads[:, D:], kept[slots[2]], NT)).astype(BF16)


def back_kernel(
    n_main, place, info, grad_in, dq_in, own_in, recv_in, gains, scale_f, scale_a, logs, high_terms, norm_f, slope,
    norm_a, q_in, kv_own, kv_other, w_down, *refs
):
    sources = refs[:n_main]
    (
        ig_high, ig_out, dq_out, own_out, other_out, grad_res, all_terms,
        kept, sems, kv, kv_sems, grad_att, act, mask, dq, dkv, slope_in, rows_in, row_sems,
    ) = refs[n_main:]
    keys = gather_keys(kv_own, kv_other, info[1], kv, kv_sems)
    terms = all_terms.at[0]
    all_terms[1] = high_terms[...]
    slope_copy = pltpu.make_async_copy(slope, slope_in, row_sems.at[3])
    copies = [
        pltpu.make_async_copy(array, rows_in.at[i], row_sems.at[i])
        for i, array in enumerate((norm_f, norm_a, q_in))
    ]
    loads = Loads(place, sources, w_down, kept, sems)
    wait, step = (loads.wait, loads.step)
    loads.main(2, (9, 0), (10, 1), (11, 2))
    loads.copies(copies[0], slope_copy)
    loads.down(0, 5, 0)
    loads.main(1, (1, 0))
    for block in (1, 2, 3):
        loads.down(0, 5 + block, block)
        loads.main(1, (1 + block, block))
    loads.main(0, (0, 3))
    loads.copies(*keys, *copies[1:])
    step(3)
    fill_mask(mask, info[0])
    step()
    ig_high[...] = input_grad(grad_in, dq_in, own_in, recv_in, kept, (9, 10, 11), wait, step)
    grad_float = ig_high[...].astype(F32)
    copies[0].wait()
    grad_now = norm_backward(grad_float, rows_in[0].astype(F32), scale_f[:, 0:1], gains[1:2, :])
    terms[8:9, :] = jnp.sum(grad_now, axis=0, keepdims=True)
    terms[9:10, :] = jnp.sum(grad_float, axis=0, keepdims=True)
    slope_copy.wait()
    total = feed_backward(
        grad_now.astype(BF16), slope_in, (1, 2, 3, 4), (5, 6, 7, 8), kept, act, terms, wait, lambda: step(2)
    )
    ig_out[...] = (grad_now + total).astype(BF16)
    step(8)
    wait(0)
    for copy in (*keys, *copies[1:]):
        copy.wait()
    start_attention_backward(
        ig_out[...], rows_in[1], scale_a[:, 0:1], gains[0:1, :], kept[0], grad_res, grad_att, terms
    )
    attend_backward(grad_att, rows_in.at[2], kv, logs, mask, dq, dkv)
    finish_attention_backward(info[1], dq, dkv, dq_out, own_out, other_out, terms)


def last_kernel(n_main, place, info, grad_res, dq_in, own_in, recv_in, ig_one, ig_two, ig_three, w_down, *refs):
    sources = refs[:n_main]
    *outs, kept, sems = refs[n_main:]
    loads = Loads(place, sources, w_down, kept, sems)
    loads.main(0, (0, 0), (1, 1), (2, 2))
    loads.step(3)
    for section, grads in ((1, ig_one), (2, ig_two), (3, ig_three)):
        for bits, out in enumerate(outs):

            @pl.when(info[2] == section ^ bits)
            def _():
                out[...] = grads[...]

    grads = input_grad(grad_res, dq_in, own_in, recv_in, kept, (0, 1, 2), loads.wait, loads.step)
    for bits, out in enumerate(outs):

        @pl.when(info[2] == bits)
        def _():
            out[...] = grads


def launch(kernel, name, work, outs, scratch, smem, vmem, hbm):
    return pl.pallas_call(
        functools.partial(kernel, len(hbm[1])),
        name=name,
        out_shape=outs,
        in_specs=[IN_SMEM] * len(smem)
        + [IN_VMEM] * len(vmem)
        + [IN_HBM] * (len(hbm[0]) + len(hbm[1])),
        out_specs=[IN_VMEM] * len(outs),
        scratch_shapes=scratch,
        cost_estimate=pl.CostEstimate(flops=int(work * 1e9), bytes_accessed=2**20, transcendentals=0),
        compiler_params=pltpu.CompilerParams(vmem_limit_bytes=58 * 2**20),
    )(*smem, *vmem, *hbm[0], *hbm[1])


def main_slots(count):
    return [pltpu.VMEM((count, D, D), BF16), pltpu.SemaphoreType.DMA((count,))]


def flip(value, axis, bit):
    count = lax.axis_size(axis)
    return lax.ppermute(value, axis, [(source, source ^ bit) for source in range(count)])


def tied(value, *others):
    return lax.optimization_barrier((value, *others))[0]


def split_three(value):
    high = lax.optimization_barrier(value.astype(BF16))
    rest = value - high.astype(F32)
    middle = lax.optimization_barrier(rest.astype(BF16))
    low = (rest - middle.astype(F32)).astype(BF16)
    return jnp.concatenate([high.reshape(-1, D), middle.reshape(-1, D), low.reshape(-1, D)])


def join_three(rows):
    parts = rows.astype(F32).reshape(3, -1)
    return parts[0] + parts[1] + parts[2]


def tied(values, *others):
    return lax.optimization_barrier((*values, *others))[: len(values)]


def gather_weights(own, base, small, early, finish):
    over_x = lambda value: flip(value, "section", 1)
    over_y = lambda value: flip(value, "section", 2)
    over_z = lambda value: flip(value, "dp", 2)
    over_core = lambda value: flip(value, "dp", 1)
    extra = split_three(small)
    first = lax.dynamic_slice(own, (0, base * D), (HALF + EXTRA, D))
    first = lax.dynamic_update_slice(lax.optimization_barrier(first), extra, (HALF, 0))
    x_one, y_one = (over_x(first), over_y(first))

    second = lax.dynamic_slice(own, (HALF, base * D), (HALF, D))
    far = lax.dynamic_slice(own, (HALF + QUARTER, (base ^ 1) * D), (QUARTER, D))
    early = early(second)
    x_now, y_now, second = tied((x_one, y_one, second), *early)
    x_two, y_two, xz_one = (over_x(second), over_y(second), over_z(x_now[:HALF]))
    xc_one, yc_one = (over_core(x_now[:HALF]), over_core(y_now[:HALF]))

    x_now, y_now, z_now, relay = tied((x_two, y_two, xz_one, y_one), xc_one, yc_one)
    d_one, dz_one, xz_two = (over_x(relay), over_y(z_now), over_z(x_now))
    xc_two, yc_two = (over_core(x_now), over_core(y_now))

    rows = extra.shape[0]
    smalls = jnp.stack([small] + [join_three(piece[HALF : HALF + rows]) for piece in (x_one, y_one, d_one)])
    d_now, dz_now, z_now, relay, left, far, z_one = tied(
        (d_one, dz_one, xz_two, y_two, y_one, far, xz_one), xc_two, yc_two
    )
    smalls = finish(smalls)
    d_two = over_x(relay)
    mixed_y = over_y(jnp.concatenate([z_now, far]))
    mixed_z = over_z(jnp.concatenate([left[:HALF], relay[:QUARTER]]))
    xzc_one, xzc_two = (over_core(z_one), over_core(z_now))
    dc_one, dzc_one = (over_core(d_now[:HALF]), over_core(dz_now))

    d_now, y_now, z_now = tied((d_two, mixed_y, mixed_z), xzc_one, xzc_two, dc_one, dzc_one, *smalls)
    dc_two, mixed_yc, mixed_zc = (over_core(d_now), over_core(y_now), over_core(z_now))
    received = (
        x_one, x_two, xz_one, xz_two, xc_one, xc_two, xzc_one, xzc_two,
        y_one, y_two, mixed_z, mixed_y, yc_one, yc_two, mixed_zc, mixed_yc,
        d_one, d_two, dz_one, dc_one, dc_two, dzc_one,
    )
    return (list(received), smalls, early)


def butterfly_steps():
    steps = {}
    for axis in ("dp", "section"):
        bits = []
        while 2 ** len(bits) < lax.axis_size(axis):
            bits.append(2 ** len(bits))
        steps[axis] = [(axis, bit) for bit in bits]
    return steps["section"][:1] + steps["dp"] + steps["section"][1:]


def choose(values, index):
    low = jnp.where(index % 2 == 0, values[0], values[1])
    high = jnp.where(index % 2 == 0, values[2], values[3])
    return jnp.where(index < 2, low, high)


def pick(stack, index):
    return lax.dynamic_index_in_dim(stack, index, 0, keepdims=False)


def spread(mine, got_x, got_y, got_d, section, core):
    same = core == section % 2
    keep_first = jnp.where(same, mine, got_x)
    keep_second = jnp.where(same, got_y, got_d)
    send = jnp.stack([jnp.where(same, got_x, mine), jnp.where(same, got_d, got_y)])
    got = flip(send, "dp", 1)
    batch = section // 2
    kept_rows = [jnp.where(batch == 0, keep_first, keep_second), jnp.where(batch == 0, keep_second, keep_first)]
    got_rows = [jnp.where(batch == 0, got[0], got[1]), jnp.where(batch == 0, got[1], got[0])]
    parts = []
    for kept_now, got_now in zip(kept_rows, got_rows):
        parts.append(
            jnp.concatenate(
                [jnp.where(core == 0, kept_now, got_now), jnp.where(core == 0, got_now, kept_now)]
            )
        )
    return jnp.stack(parts)[None, :, None]


def per_device(inputs_x, lengths, w_main, w_down, gains, bias_main, bias_down, cotangent):
    section = lax.axis_index("section")
    lane = lax.axis_index("dp")
    core, plane = (lane % 2, (lane // 2) % 2)
    base = core * 2 + plane
    rows = inputs_x.shape[2] // 2

    batch = section // 2
    same = core == section % 2
    blocks = jnp.arange(4, dtype=jnp.int32)[None, :]
    away = section ^ jnp.arange(4, dtype=jnp.int32)[:, None]

    def take_inputs(after):
        tied_x, tied_grad, tied_lengths, _ = lax.optimization_barrier((inputs_x, cotangent, lengths, after))
        lines = jnp.stack([pick(tied_x[:, 0], batch), pick(tied_grad[:, 0], batch)])
        mine = lax.dynamic_slice_in_dim(lines, core * rows, rows, axis=1)
        other = flip(lax.dynamic_slice_in_dim(lines, (1 - core) * rows, rows, axis=1), "dp", 1)
        mine = jnp.where(same, mine, other)
        length_own = lax.dynamic_slice_in_dim(tied_lengths[:, 0], batch, 1).astype(F32)
        length_other = flip(jnp.broadcast_to(length_own[None], (8, 128)), "dp", 1)[0, :1]
        length = jnp.where(same, length_own, length_other).astype(jnp.int32)
        info = jnp.concatenate([length, core[None].astype(jnp.int32), section[None].astype(jnp.int32)])
        place = jnp.where(away == 0, 0, 1 + (away - 1) * 4 + (blocks ^ base)).astype(jnp.int32)
        return (mine[0], mine[1], info, place)

    small = jnp.concatenate([gains, bias_main], axis=1).reshape(-1)
    own = w_main[0]

    def take_smalls(smalls):
        smalls = jnp.stack([pick(smalls, section ^ s) for s in range(4)])
        return (smalls[:, :D], smalls[:, D:], bias_down.reshape(4, D))

    received, smalls, early = gather_weights(own, base, small, take_inputs, take_smalls)
    hidden, grad_last, info, place = early
    all_gains, all_bias, down_bias = smalls
    sources = [own] + received

    def row(width, kind):
        return SHAPE((rows, width), kind)

    pair_sems = pltpu.SemaphoreType.DMA((2,))
    keys = pltpu.VMEM((2 * rows, 2 * D), BF16)
    q0, kv0 = launch(
        first_kernel, "first", 5, [row(D, BF16), row(2 * D, BF16)], main_slots(3),
        [place], [hidden, all_bias], ([w_down], sources),
    )
    kv0_other = flip(kv0, "dp", 1)
    hs0, hs1, q2, kv2, logs0, norm0, scale0, norm1, scale1, slope1 = launch(
        low_kernel, "low", 20,
        [
            row(D, BF16), row(D, BF16), row(D, BF16), row(2 * D, BF16), SHAPE((128, rows), F32),
            row(D, BF16), row(128, F32), row(D, BF16), row(128, F32), row(FF, BF16),
        ],
        main_slots(12)
        + [keys, pair_sems, pltpu.VMEM((rows, D), BF16), pltpu.VMEM((rows, FF), BF16)],
        [place, info], [hidden, q0, all_bias, down_bias, all_gains, kv0, kv0_other], ([w_down], sources),
    )
    kv2_other = flip(kv2, "dp", 1)
    hs2, hs3, ig3, dq2, own2, other2, res2, terms2 = launch(
        high_kernel, "high", 32,
        [
            row(D, BF16), row(D, BF16), row(D, BF16), row(D, BF16), row(2 * D, BF16), row(2 * D, BF16),
            row(D, F32), SHAPE((10, D), F32),
        ],
        main_slots(9)
        + [
            keys, pair_sems, pltpu.VMEM((rows, D), BF16), pltpu.VMEM((rows, FF), BF16),
            pltpu.VMEM((rows, FF), BF16), pltpu.VMEM((2 * rows, rows), F32), pltpu.VMEM((128, rows), F32),
            pltpu.VMEM((rows, D), BF16), pltpu.VMEM((rows, D), F32), pltpu.VMEM((2 * rows, 2 * D), F32),
        ],
        [place, info], [hs1, q2, grad_last, all_bias, down_bias, all_gains, kv2, kv2_other],
        ([w_down], sources),
    )
    recv2 = flip(other2, "dp", 1)
    ig2, ig1, dq0, own0, other0, res0, terms = launch(
        back_kernel, "back", 20,
        [
            row(D, BF16), row(D, BF16), row(D, BF16), row(2 * D, BF16), row(2 * D, BF16), row(D, F32),
            SHAPE((2, 10, D), F32),
        ],
        main_slots(12)
        + [
            keys, pair_sems, pltpu.VMEM((rows, D), BF16), pltpu.VMEM((rows, FF), BF16),
            pltpu.VMEM((2 * rows, rows), F32), pltpu.VMEM((rows, D), F32), pltpu.VMEM((2 * rows, 2 * D), F32),
            pltpu.VMEM((rows, FF), BF16), pltpu.VMEM((3, rows, D), BF16), pltpu.SemaphoreType.DMA((4,)),
        ],
        [place, info],
        [res2, dq2, own2, recv2, all_gains, scale1, scale0, logs0, terms2],
        ([norm1, slope1, norm0, q0, kv0, kv0_other, w_down], sources),
    )
    outputs = [choose((hs0, hs1, hs2, hs3), section ^ bits) for bits in range(4)]
    outputs = [outputs[0]] + [flip(outputs[bits], "section", bits) for bits in (1, 2, 3)]
    other0, terms, res0, *outputs = tied((other0, terms, res0, *outputs))
    recv0 = flip(other0, "dp", 1)
    first_step, *middle_steps, last_step = butterfly_steps()
    got = flip(terms, *first_step)
    grads = launch(
        last_kernel, "last", 5, [row(D, BF16)] * 4, main_slots(3), [place, info],
        [res0, dq0, own0, recv0, ig1, ig2, ig3], ([w_down], sources),
    )
    terms, got, *grads = tied((terms, got, *grads))
    terms = terms + got
    moved = [flip(grads[bits], "section", bits) for bits in (1, 2, 3)]
    for axis, bit in middle_steps:
        terms = terms + flip(terms, axis, bit)
    terms, *moved = tied((terms, *moved))
    terms = terms + flip(terms, *last_step)
    hidden_states = spread(*outputs, section, core)
    input_grads = spread(grads[0], *moved, section, core)
    grad_main = terms[:, :8].reshape(4, FF)
    return (hidden_states, input_grads, grad_main, terms[:, 8:])


def solution(mesh):
    placed = (
        P(None, "dp", None, None),
        P(None, "dp"),
        P("section", None, None),
        P(),
        P("section", None),
        P("section", None),
        P(),
        P(None, "dp", None, None),
    )
    return jax.shard_map(
        per_device,
        mesh=mesh,
        in_specs=placed,
        out_specs=(
            P("section", None, "dp", None, None),
            P("section", None, "dp", None, None),
            P(),
            P(),
        ),
        check_vma=False,
    )
```

```python
import functools

import jax
import jax.numpy as jnp
from jax import lax
from jax.experimental import pallas as pl
from jax.experimental.pallas import tpu as pltpu
from jax.sharding import PartitionSpec as P

D = 1024
HEADS = 16
HEAD = 64
FF = 4096
EPSILON = 1e-12
NEGATIVE = -1e30
EXTRA = 16

F32, BF16 = (jnp.float32, jnp.bfloat16)
NN = (((1,), (0,)), ((), ()))
NT = (((1,), (1,)), ((), ()))
TN = (((0,), (0,)), ((), ()))
IN_VMEM = pl.BlockSpec(memory_space=pltpu.VMEM)
IN_SMEM = pl.BlockSpec(memory_space=pltpu.SMEM)
IN_HBM = pl.BlockSpec(memory_space=pl.ANY)
SHAPE = jax.ShapeDtypeStruct


def dot(left, right, dims=NN):
    return lax.dot_general(left, right, dims, preferred_element_type=F32)


ONE, TWO, MIDDLE = (448, 576, 256)
LATE = TWO - MIDDLE
PIECES = (
    ((1, 0, 0, ONE), (2, 0, ONE, TWO)),
    ((3, 0, 0, ONE), (4, 0, ONE, TWO)),
    ((5, 0, 0, ONE), (6, 0, ONE, TWO)),
    ((6, TWO, 0, ONE), (7, 0, ONE, TWO)),
    ((8, 0, 0, ONE), (9, 0, ONE, TWO)),
    ((10, 0, 0, ONE + MIDDLE), (9, TWO, ONE + MIDDLE, LATE)),
    ((5, ONE, 0, ONE), (11, 0, ONE, TWO)),
    ((12, 0, 0, ONE + MIDDLE), (11, TWO, ONE + MIDDLE, LATE)),
    ((13, 0, 0, ONE), (14, 0, ONE, TWO)),
    ((15, 0, 0, ONE), (16, 0, ONE, TWO)),
    ((17, 0, 0, ONE), (18, 0, ONE, TWO)),
    ((19, 0, 0, ONE), (20, 0, ONE, TWO)),
)


def fetch_main(place, row, sources, blocks, kept, sems):
    for slot, block in blocks:

        @pl.when(place[row, block] == 0)
        def _():
            pltpu.make_async_copy(
                sources[0].at[:, pl.ds(block * D, D)], kept.at[slot], sems.at[slot]
            ).start()

        for which, pieces in enumerate(PIECES):

            @pl.when(place[row, block] == 1 + which)
            def _():
                for source, at, to, rows in pieces:
                    pltpu.make_async_copy(
                        sources[source].at[pl.ds(at, rows), :],
                        kept.at[slot, pl.ds(to, rows), :],
                        sems.at[slot],
                    ).start()


def fetch_down(w_down, layer, block, kept, slot, sems):
    pltpu.make_async_copy(
        w_down.at[layer, pl.ds(block * D, D), :], kept.at[slot], sems.at[slot]
    ).start()


def wait_slot(w_down, kept, slot, sems):
    pltpu.make_async_copy(w_down.at[0, pl.ds(0, D), :], kept.at[slot], sems.at[slot]).wait()


def norm_forward(residual, gain, shift):
    center = residual - jnp.mean(residual, axis=1, keepdims=True)
    scale = lax.rsqrt(jnp.mean(center * center, axis=1, keepdims=True) + EPSILON)
    normed = center * scale
    return ((normed * gain + shift).astype(BF16), normed.astype(BF16), scale)


def norm_backward(grad, normed, scale, gain):
    up = grad * gain
    first = jnp.mean(up, axis=1, keepdims=True)
    second = jnp.mean(up * normed, axis=1, keepdims=True)
    return (up - first - normed * second) * scale


def lane_halves():
    lane = lax.broadcasted_iota(jnp.int32, (1, 128), 1)
    return (lane < HEAD, lane >= HEAD)


def project(hidden, biases, kept, slots, q_out, kv_out, wait):
    wait(slots[0])
    queries = (dot(hidden, kept[slots[0]]) + biases[:, :D]).astype(BF16)
    q_out[...] = queries * BF16(HEAD ** (-0.5))
    wait(slots[1])
    kv_out[:, :D] = dot(hidden, kept[slots[1]]).astype(BF16)
    wait(slots[2])
    kv_out[:, D:] = (dot(hidden, kept[slots[2]]) + biases[:, D : 2 * D]).astype(BF16)


def attend(q_ref, kv, length, attended, log_out, step):
    rows, keys = (q_ref.shape[0], kv.shape[0])
    position = lax.broadcasted_iota(jnp.int32, (1, keys), 1)
    mask = jnp.where(position < length, 0.0, NEGATIVE).astype(F32)
    halves = lane_halves()
    lane = lax.broadcasted_iota(jnp.int32, (1, 128), 1)
    tops = jnp.zeros((rows, 128), F32)
    sums = jnp.ones((rows, 128), F32)
    for pair in range(HEADS // 2):
        step()
        at = slice(pair * 128, pair * 128 + 128)
        keys_pair, values_pair, queries = (kv[:, at], kv[:, D + at.start : D + at.stop], q_ref[:, at])
        parts = []
        for which in range(2):
            mine = halves[which]
            scores = dot(jnp.where(mine, queries, BF16(0)), keys_pair, NT) + mask
            top = jnp.max(scores, axis=1, keepdims=True)
            powers = jnp.exp(scores - top).astype(BF16)
            both = dot(powers, jnp.where(mine, values_pair, BF16(1)))
            parts.append(both * (1.0 / pltpu.roll(both, HEAD, 1)))
            place = lane == (HEAD * (1 - which) + pair)
            tops = jnp.where(place, top, tops)
            sums = jnp.where(place, both, sums)
        attended[:, at] = jnp.where(halves[0], parts[0], parts[1]).astype(BF16)
    log_out[...] = (tops + jnp.log(sums)).T


def attend_backward(grad_att, q_ref, kv, log_ref, mask, dq_out, dkv):
    halves = lane_halves()
    for pair in range(HEADS // 2):
        at = slice(pair * 128, pair * 128 + 128)
        low = slice(D + at.start, D + at.stop)
        keys_pair, values_pair, queries, grads = (kv[:, at], kv[:, low], q_ref[:, at], grad_att[:, at])
        grad_q = grad_k = grad_v = None
        for which in range(2):
            mine = halves[which]
            q_mine = jnp.where(mine, queries, BF16(0))
            g_mine = jnp.where(mine, grads, BF16(0))
            row = HEAD * (1 - which) + pair
            scores = dot(keys_pair, q_mine, NT) + mask[...]
            soft = jnp.exp(scores - log_ref[row : row + 1, :])
            grad_soft = dot(values_pair, g_mine, NT)
            total = jnp.sum(soft * grad_soft, axis=0, keepdims=True)
            grad_scores = (soft * (grad_soft - total)).astype(BF16)
            part_v = dot(soft.astype(BF16), g_mine)
            part_k = dot(grad_scores, q_mine)
            part_q = dot(grad_scores, jnp.where(mine, keys_pair, BF16(0)), TN)
            grad_v = part_v if which == 0 else grad_v + part_v
            grad_k = part_k if which == 0 else grad_k + part_k
            grad_q = part_q if which == 0 else grad_q + part_q
        dq_out[:, at] = grad_q * HEAD ** (-0.5)
        dkv[:, at] = grad_k
        dkv[:, low] = grad_v


def gelu_pair(value):
    below = 0.5 + 0.5 * lax.erf(value * 0.7071067811865476)
    return (value * below, below + value * (0.3989422804014327 * jnp.exp(value * value * -0.5)))


def feed_forward(hidden, biases, first_slots, second_slots, kept, act, slope, wait, step):
    total = None
    for block in range(4):
        step()
        wait(first_slots[block])
        full = slice(block * D, block * D + D)
        value, grad = gelu_pair(dot(hidden, kept[first_slots[block]]) + biases[:, full])
        slope[:, full] = grad.astype(BF16)
        act[:, full] = value.astype(BF16)
        wait(second_slots[block])
        part = dot(act[:, full], kept[second_slots[block]])
        total = part if total is None else total + part
    return total


def feed_backward(grad_low, slope, first_slots, second_slots, kept, act, terms, wait, step):
    total = None
    for block in range(4):
        step()
        full = slice(block * D, block * D + D)
        wait(second_slots[block])
        grad = dot(grad_low, kept[second_slots[block]], NT) * slope[:, full].astype(F32)
        terms[4 + block : 5 + block, :] = jnp.sum(grad, axis=0, keepdims=True)
        act[:, full] = grad.astype(BF16)
        wait(first_slots[block])
        part = dot(act[:, full], kept[first_slots[block]], NT)
        total = part if total is None else total + part
    return total


def gather_keys(kv_own, kv_other, half, kv, sems):
    rows = kv_own.shape[0]
    mine = pltpu.make_async_copy(kv_own, kv.at[pl.ds(pl.multiple_of(half * rows, rows), rows), :], sems.at[0])
    other = pltpu.make_async_copy(
        kv_other, kv.at[pl.ds(pl.multiple_of((1 - half) * rows, rows), rows), :], sems.at[1]
    )
    return (mine, other)


class Loads:
    def __init__(self, place, sources, w_down, kept, sems):
        self.place, self.sources, self.w_down, self.kept, self.sems = (place, sources, w_down, kept, sems)
        self.starts = []

    def main(self, section, *slots):
        for slot, block in slots:
            self.starts.append(
                lambda slot=slot, block=block: fetch_main(
                    self.place, section, self.sources, ((slot, block),), self.kept, self.sems
                )
            )

    def down(self, layer, slot, block):
        self.starts.append(lambda: fetch_down(self.w_down, layer, block, self.kept, slot, self.sems))

    def copies(self, *copies):
        self.starts.append(lambda: [copy.start() for copy in copies])

    def step(self, count=1):
        for _ in range(count):
            if self.starts:
                self.starts.pop(0)()

    def wait(self, slot):
        wait_slot(self.w_down, self.kept, slot, self.sems)


def first_kernel(n_main, place, hidden, main_bias, w_down, *refs):
    sources = refs[:n_main]
    q_out, kv_out, kept, sems = refs[n_main:]
    loads = Loads(place, sources, w_down, kept, sems)
    loads.main(0, (0, 0), (1, 1), (2, 2))
    loads.step(3)
    project(hidden[...], main_bias[0:1, :], kept, (0, 1, 2), q_out, kv_out, loads.wait)


def low_kernel(n_main, place, info, hidden, q_in, main_bias, down_bias, gains, kv_own, kv_other, w_down, *refs):
    sources = refs[:n_main]
    (
        mid_out, out_out, q_out, kv_out, log_out, norm_a, scale_a, norm_f, scale_f, slope,
        kept, sems, kv, kv_sems, attended, act,
    ) = refs[n_main:]
    keys = gather_keys(kv_own, kv_other, info[1], kv, kv_sems)
    loads = Loads(place, sources, w_down, kept, sems)
    wait, step = (loads.wait, loads.step)
    loads.copies(*keys)
    loads.main(0, (0, 3))
    for block in range(4):
        loads.main(1, (1 + block, block))
        loads.down(0, 5 + block, block)
    loads.main(2, (9, 0), (10, 1), (11, 2))
    step(2)
    for key in keys:
        key.wait()
    attend(q_in, kv, info[0], attended, log_out, step)
    wait(0)
    residual = hidden[...].astype(F32) + dot(attended[...], kept[0]) + main_bias[0:1, 2 * D : 3 * D]
    mid, norm, scale = norm_forward(residual, gains[0:1, :], main_bias[0:1, 3 * D :])
    mid_out[...] = mid
    norm_a[...] = norm
    scale_a[...] = jnp.broadcast_to(scale, scale_a.shape)
    hidden_now = mid_out[...]
    total = feed_forward(
        hidden_now, main_bias[1:2, :], (1, 2, 3, 4), (5, 6, 7, 8), kept, act, slope, wait, step
    )
    residual = mid_out[...].astype(F32) + total + down_bias[0:1, :]
    out, norm, scale = norm_forward(residual, gains[1:2, :], down_bias[1:2, :])
    out_out[...] = out
    norm_f[...] = norm
    scale_f[...] = jnp.broadcast_to(scale, scale_f.shape)
    project(out_out[...], main_bias[2:3, :], kept, (9, 10, 11), q_out, kv_out, wait)


def start_attention_backward(grad, norm, scale, gain, w_out, grad_res, grad_att, terms):
    grad_float = grad.astype(F32)
    grad_now = norm_backward(grad_float, norm.astype(F32), scale, gain)
    grad_res[...] = grad_now
    terms[2:3, :] = jnp.sum(grad_now, axis=0, keepdims=True)
    terms[3:4, :] = jnp.sum(grad_float, axis=0, keepdims=True)
    grad_att[...] = dot(grad_now.astype(BF16), w_out, NT).astype(BF16)


def finish_attention_backward(half, dq, dkv, dq_out, own_out, other_out, terms):
    rows = dq.shape[0]
    grad_q = dq[...]
    dq_out[...] = grad_q.astype(BF16)
    terms[0:1, :] = jnp.sum(grad_q, axis=0, keepdims=True)
    terms[1:2, :] = jnp.sum(dkv[:, D:], axis=0, keepdims=True)
    own_out[...] = dkv[pl.ds(pl.multiple_of(half * rows, rows), rows), :].astype(BF16)
    other_out[...] = dkv[pl.ds(pl.multiple_of((1 - half) * rows, rows), rows), :].astype(BF16)


def fill_mask(mask, length):
    position = lax.broadcasted_iota(jnp.int32, mask.shape, 0)
    mask[...] = jnp.where(position < length, 0.0, NEGATIVE).astype(F32)


def high_kernel(n_main, place, info, hidden, q_in, cotangent, main_bias, down_bias, gains, kv_own, kv_other, w_down, *refs):
    sources = refs[:n_main]
    (
        mid_out, out_out, ig_out, dq_out, own_out, other_out, grad_res, terms,
        kept, sems, kv, kv_sems, attended, act, slope, mask, logs, norm_a, dq, dkv,
    ) = refs[n_main:]
    keys = gather_keys(kv_own, kv_other, info[1], kv, kv_sems)
    loads = Loads(place, sources, w_down, kept, sems)
    wait, step = (loads.wait, loads.step)
    loads.copies(*keys)
    loads.main(2, (0, 3))
    for block in range(4):
        loads.main(3, (1 + block, block))
        loads.down(1, 5 + block, block)
    done = lambda slot: None
    step(2)
    fill_mask(mask, info[0])
    for key in keys:
        key.wait()
    attend(q_in, kv, info[0], attended, logs, step)
    wait(0)
    residual = hidden[...].astype(F32) + dot(attended[...], kept[0]) + main_bias[2:3, 2 * D : 3 * D]
    mid, norm, scale_mid = norm_forward(residual, gains[2:3, :], main_bias[2:3, 3 * D :])
    mid_out[...] = mid
    norm_a[...] = norm
    hidden_now = mid_out[...]
    total = feed_forward(
        hidden_now, main_bias[3:4, :], (1, 2, 3, 4), (5, 6, 7, 8), kept, act, slope, wait, step
    )
    residual = mid_out[...].astype(F32) + total + down_bias[2:3, :]
    out, norm, scale = norm_forward(residual, gains[3:4, :], down_bias[3:4, :])
    out_out[...] = out
    grad_float = cotangent[...].astype(F32)
    grad_now = norm_backward(grad_float, norm.astype(F32), scale, gains[3:4, :])
    terms[8:9, :] = jnp.sum(grad_now, axis=0, keepdims=True)
    terms[9:10, :] = jnp.sum(grad_float, axis=0, keepdims=True)
    total = feed_backward(
        grad_now.astype(BF16), slope, (1, 2, 3, 4), (5, 6, 7, 8), kept, act, terms, done, step
    )
    ig_out[...] = (grad_now + total).astype(BF16)
    start_attention_backward(
        ig_out[...], norm_a[...], scale_mid, gains[2:3, :], kept[0], grad_res, attended, terms
    )
    attend_backward(attended, q_in, kv, logs, mask, dq, dkv)
    finish_attention_backward(info[1], dq, dkv, dq_out, own_out, other_out, terms)


def input_grad(grad_res, dq_in, own_in, recv_in, kept, slots, wait, step):
    wait(slots[0])
    step()
    total = grad_res[...] + dot(dq_in[...], kept[slots[0]], NT)
    grads = (own_in[...].astype(F32) + recv_in[...].astype(F32)).astype(BF16)
    wait(slots[1])
    step()
    total = total + dot(grads[:, :D], kept[slots[1]], NT)
    wait(slots[2])
    step()
    return (total + dot(grads[:, D:], kept[slots[2]], NT)).astype(BF16)


def back_kernel(
    n_main, place, info, grad_in, dq_in, own_in, recv_in, gains, scale_f, scale_a, logs, high_terms, norm_f, slope,
    norm_a, q_in, kv_own, kv_other, w_down, *refs
):
    sources = refs[:n_main]
    (
        ig_high, ig_out, dq_out, own_out, other_out, grad_res, all_terms,
        kept, sems, kv, kv_sems, grad_att, act, mask, dq, dkv, slope_in, rows_in, row_sems,
    ) = refs[n_main:]
    keys = gather_keys(kv_own, kv_other, info[1], kv, kv_sems)
    terms = all_terms.at[0]
    all_terms[1] = high_terms[...]
    slope_copy = pltpu.make_async_copy(slope, slope_in, row_sems.at[3])
    copies = [
        pltpu.make_async_copy(array, rows_in.at[i], row_sems.at[i])
        for i, array in enumerate((norm_f, norm_a, q_in))
    ]
    loads = Loads(place, sources, w_down, kept, sems)
    wait, step = (loads.wait, loads.step)
    loads.main(2, (9, 0), (10, 1), (11, 2))
    loads.copies(copies[0], slope_copy)
    loads.down(0, 5, 0)
    loads.main(1, (1, 0))
    for block in (1, 2, 3):
        loads.down(0, 5 + block, block)
        loads.main(1, (1 + block, block))
    loads.main(0, (0, 3))
    loads.copies(*keys, *copies[1:])
    step(3)
    fill_mask(mask, info[0])
    step()
    ig_high[...] = input_grad(grad_in, dq_in, own_in, recv_in, kept, (9, 10, 11), wait, step)
    grad_float = ig_high[...].astype(F32)
    copies[0].wait()
    grad_now = norm_backward(grad_float, rows_in[0].astype(F32), scale_f[:, 0:1], gains[1:2, :])
    terms[8:9, :] = jnp.sum(grad_now, axis=0, keepdims=True)
    terms[9:10, :] = jnp.sum(grad_float, axis=0, keepdims=True)
    slope_copy.wait()
    total = feed_backward(
        grad_now.astype(BF16), slope_in, (1, 2, 3, 4), (5, 6, 7, 8), kept, act, terms, wait, lambda: step(2)
    )
    ig_out[...] = (grad_now + total).astype(BF16)
    step(8)
    wait(0)
    for copy in (*keys, *copies[1:]):
        copy.wait()
    start_attention_backward(
        ig_out[...], rows_in[1], scale_a[:, 0:1], gains[0:1, :], kept[0], grad_res, grad_att, terms
    )
    attend_backward(grad_att, rows_in.at[2], kv, logs, mask, dq, dkv)
    finish_attention_backward(info[1], dq, dkv, dq_out, own_out, other_out, terms)


def last_kernel(n_main, place, info, grad_res, dq_in, own_in, recv_in, ig_one, ig_two, ig_three, w_down, *refs):
    sources = refs[:n_main]
    *outs, kept, sems = refs[n_main:]
    loads = Loads(place, sources, w_down, kept, sems)
    loads.main(0, (0, 0), (1, 1), (2, 2))
    loads.step(3)
    for section, grads in ((1, ig_one), (2, ig_two), (3, ig_three)):
        for bits, out in enumerate(outs):

            @pl.when(info[2] == section ^ bits)
            def _():
                out[...] = grads[...]

    grads = input_grad(grad_res, dq_in, own_in, recv_in, kept, (0, 1, 2), loads.wait, loads.step)
    for bits, out in enumerate(outs):

        @pl.when(info[2] == bits)
        def _():
            out[...] = grads


def launch(kernel, name, work, outs, scratch, smem, vmem, hbm):
    return pl.pallas_call(
        functools.partial(kernel, len(hbm[1])),
        name=name,
        out_shape=outs,
        in_specs=[IN_SMEM] * len(smem)
        + [IN_VMEM] * len(vmem)
        + [IN_HBM] * (len(hbm[0]) + len(hbm[1])),
        out_specs=[IN_VMEM] * len(outs),
        scratch_shapes=scratch,
        cost_estimate=pl.CostEstimate(flops=int(work * 1e9), bytes_accessed=2**20, transcendentals=0),
        compiler_params=pltpu.CompilerParams(vmem_limit_bytes=58 * 2**20),
    )(*smem, *vmem, *hbm[0], *hbm[1])


def main_slots(count):
    return [pltpu.VMEM((count, D, D), BF16), pltpu.SemaphoreType.DMA((count,))]


def flip(value, axis, bit):
    count = lax.axis_size(axis)
    return lax.ppermute(value, axis, [(source, source ^ bit) for source in range(count)])


def tied(value, *others):
    return lax.optimization_barrier((value, *others))[0]


def split_three(value):
    high = lax.optimization_barrier(value.astype(BF16))
    rest = value - high.astype(F32)
    middle = lax.optimization_barrier(rest.astype(BF16))
    low = (rest - middle.astype(F32)).astype(BF16)
    return jnp.concatenate([high.reshape(-1, D), middle.reshape(-1, D), low.reshape(-1, D)])


def join_three(rows):
    parts = rows.astype(F32).reshape(3, -1)
    return parts[0] + parts[1] + parts[2]


def tied(values, *others):
    return lax.optimization_barrier((*values, *others))[: len(values)]


def gather_weights(own, base, small, early, finish):
    over_x = lambda value: flip(value, "section", 1)
    over_y = lambda value: flip(value, "section", 2)
    over_z = lambda value: flip(value, "dp", 2)
    over_core = lambda value: flip(value, "dp", 1)
    extra = split_three(small)
    first = lax.dynamic_slice(own, (0, base * D), (ONE + EXTRA, D))
    first = lax.dynamic_update_slice(lax.optimization_barrier(first), extra, (ONE, 0))
    second = lax.dynamic_slice(own, (ONE, base * D), (TWO, D))
    far = lax.dynamic_slice(own, (ONE + MIDDLE, (base ^ 1) * D), (LATE, D))
    x_one, y_one, x_two = (over_x(first), over_y(first), over_x(second))
    y_two = over_y(jnp.concatenate([second, far]))
    early = early(first)

    x_first, y_first = tied((x_one, y_one))
    xz_one, d_one = (over_z(x_first[:ONE]), over_x(y_first))
    ones = jnp.concatenate([x_first[:ONE], y_first[:ONE]])

    x_second, z_now, ones = tied((x_two, xz_one, ones), *early)
    dz_one, xz_two, c_ones = (over_y(z_now), over_z(x_second), over_core(ones))
    mixed = jnp.concatenate([x_second, z_now])

    rows = extra.shape[0]
    smalls = jnp.stack([small] + [join_three(piece[ONE : ONE + rows]) for piece in (x_one, y_one, d_one)])
    y_second = y_two
    rest = jnp.concatenate([y_first[:ONE], y_second[:MIDDLE]])
    d_now, dz_now, xz_now, y_second, rest, mixed = tied((d_one, dz_one, xz_two, y_second, rest, mixed), c_ones)
    smalls = finish(smalls)
    dz_two, yz, d_two = (over_y(xz_now), over_z(rest), over_x(y_second[:TWO]))
    c_mixed, yc_two = (over_core(mixed), over_core(y_second))

    two_now, dz_last, z_now, d_now, dz_now, xz_now = tied(
        (d_two, dz_two, yz, d_now, dz_now, xz_now), c_mixed, yc_two, *smalls
    )
    dc_one, dzc_one, xzc_two = (over_core(d_now), over_core(dz_now), over_core(xz_now))
    dc_two, dzc_two, yzc = (over_core(two_now), over_core(dz_last), over_core(z_now))
    received = (
        x_one, x_two, xz_one, xz_two, c_ones, c_mixed, xzc_two, y_one, y_two, yz, yc_two, yzc,
        d_one, d_two, dz_one, dz_two, dc_one, dc_two, dzc_one, dzc_two,
    )
    return (list(received), smalls, early)


def butterfly_steps():
    steps = {}
    for axis in ("dp", "section"):
        bits = []
        while 2 ** len(bits) < lax.axis_size(axis):
            bits.append(2 ** len(bits))
        steps[axis] = [(axis, bit) for bit in bits]
    return steps["section"][:1] + steps["dp"] + steps["section"][1:]


def choose(values, index):
    low = jnp.where(index % 2 == 0, values[0], values[1])
    high = jnp.where(index % 2 == 0, values[2], values[3])
    return jnp.where(index < 2, low, high)


def pick(stack, index):
    return lax.dynamic_index_in_dim(stack, index, 0, keepdims=False)


def spread(mine, got_x, got_y, got_d, section, core):
    same = core == section % 2
    keep_first = jnp.where(same, mine, got_x)
    keep_second = jnp.where(same, got_y, got_d)
    send = jnp.stack([jnp.where(same, got_x, mine), jnp.where(same, got_d, got_y)])
    got = flip(send, "dp", 1)
    batch = section // 2
    kept_rows = [jnp.where(batch == 0, keep_first, keep_second), jnp.where(batch == 0, keep_second, keep_first)]
    got_rows = [jnp.where(batch == 0, got[0], got[1]), jnp.where(batch == 0, got[1], got[0])]
    parts = []
    for kept_now, got_now in zip(kept_rows, got_rows):
        parts.append(
            jnp.concatenate(
                [jnp.where(core == 0, kept_now, got_now), jnp.where(core == 0, got_now, kept_now)]
            )
        )
    return jnp.stack(parts)[None, :, None]


def per_device(inputs_x, lengths, w_main, w_down, gains, bias_main, bias_down, cotangent):
    section = lax.axis_index("section")
    lane = lax.axis_index("dp")
    core, plane = (lane % 2, (lane // 2) % 2)
    base = core * 2 + plane
    rows = inputs_x.shape[2] // 2

    batch = section // 2
    same = core == section % 2
    blocks = jnp.arange(4, dtype=jnp.int32)[None, :]
    away = section ^ jnp.arange(4, dtype=jnp.int32)[:, None]

    def take_inputs(after):
        tied_x, tied_grad, tied_lengths, _ = lax.optimization_barrier((inputs_x, cotangent, lengths, after))
        lines = jnp.stack([pick(tied_x[:, 0], batch), pick(tied_grad[:, 0], batch)])
        mine = lax.dynamic_slice_in_dim(lines, core * rows, rows, axis=1)
        other = flip(lax.dynamic_slice_in_dim(lines, (1 - core) * rows, rows, axis=1), "dp", 1)
        mine = jnp.where(same, mine, other)
        length_own = lax.dynamic_slice_in_dim(tied_lengths[:, 0], batch, 1).astype(F32)
        length_other = flip(jnp.broadcast_to(length_own[None], (8, 128)), "dp", 1)[0, :1]
        length = jnp.where(same, length_own, length_other).astype(jnp.int32)
        info = jnp.concatenate([length, core[None].astype(jnp.int32), section[None].astype(jnp.int32)])
        place = jnp.where(away == 0, 0, 1 + (away - 1) * 4 + (blocks ^ base)).astype(jnp.int32)
        return (mine[0], mine[1], info, place)

    small = jnp.concatenate([gains, bias_main], axis=1).reshape(-1)
    own = w_main[0]

    def take_smalls(smalls):
        smalls = jnp.stack([pick(smalls, section ^ s) for s in range(4)])
        return (smalls[:, :D], smalls[:, D:], bias_down.reshape(4, D))

    received, smalls, early = gather_weights(own, base, small, take_inputs, take_smalls)
    hidden, grad_last, info, place = early
    all_gains, all_bias, down_bias = smalls
    sources = [own] + received

    def row(width, kind):
        return SHAPE((rows, width), kind)

    pair_sems = pltpu.SemaphoreType.DMA((2,))
    keys = pltpu.VMEM((2 * rows, 2 * D), BF16)
    q0, kv0 = launch(
        first_kernel, "first", 5, [row(D, BF16), row(2 * D, BF16)], main_slots(3),
        [place], [hidden, all_bias], ([w_down], sources),
    )
    kv0_other = flip(kv0, "dp", 1)
    hs0, hs1, q2, kv2, logs0, norm0, scale0, norm1, scale1, slope1 = launch(
        low_kernel, "low", 20,
        [
            row(D, BF16), row(D, BF16), row(D, BF16), row(2 * D, BF16), SHAPE((128, rows), F32),
            row(D, BF16), row(128, F32), row(D, BF16), row(128, F32), row(FF, BF16),
        ],
        main_slots(12)
        + [keys, pair_sems, pltpu.VMEM((rows, D), BF16), pltpu.VMEM((rows, FF), BF16)],
        [place, info], [hidden, q0, all_bias, down_bias, all_gains, kv0, kv0_other], ([w_down], sources),
    )
    kv2_other = flip(kv2, "dp", 1)
    hs2, hs3, ig3, dq2, own2, other2, res2, terms2 = launch(
        high_kernel, "high", 32,
        [
            row(D, BF16), row(D, BF16), row(D, BF16), row(D, BF16), row(2 * D, BF16), row(2 * D, BF16),
            row(D, F32), SHAPE((10, D), F32),
        ],
        main_slots(9)
        + [
            keys, pair_sems, pltpu.VMEM((rows, D), BF16), pltpu.VMEM((rows, FF), BF16),
            pltpu.VMEM((rows, FF), BF16), pltpu.VMEM((2 * rows, rows), F32), pltpu.VMEM((128, rows), F32),
            pltpu.VMEM((rows, D), BF16), pltpu.VMEM((rows, D), F32), pltpu.VMEM((2 * rows, 2 * D), F32),
        ],
        [place, info], [hs1, q2, grad_last, all_bias, down_bias, all_gains, kv2, kv2_other],
        ([w_down], sources),
    )
    recv2 = flip(other2, "dp", 1)
    ig2, ig1, dq0, own0, other0, res0, terms = launch(
        back_kernel, "back", 20,
        [
            row(D, BF16), row(D, BF16), row(D, BF16), row(2 * D, BF16), row(2 * D, BF16), row(D, F32),
            SHAPE((2, 10, D), F32),
        ],
        main_slots(12)
        + [
            keys, pair_sems, pltpu.VMEM((rows, D), BF16), pltpu.VMEM((rows, FF), BF16),
            pltpu.VMEM((2 * rows, rows), F32), pltpu.VMEM((rows, D), F32), pltpu.VMEM((2 * rows, 2 * D), F32),
            pltpu.VMEM((rows, FF), BF16), pltpu.VMEM((3, rows, D), BF16), pltpu.SemaphoreType.DMA((4,)),
        ],
        [place, info],
        [res2, dq2, own2, recv2, all_gains, scale1, scale0, logs0, terms2],
        ([norm1, slope1, norm0, q0, kv0, kv0_other, w_down], sources),
    )
    outputs = [choose((hs0, hs1, hs2, hs3), section ^ bits) for bits in range(4)]
    outputs = [outputs[0]] + [flip(outputs[bits], "section", bits) for bits in (1, 2, 3)]
    other0, terms, res0, *outputs = tied((other0, terms, res0, *outputs))
    recv0 = flip(other0, "dp", 1)
    first_step, *middle_steps, last_step = butterfly_steps()
    got = flip(terms, *first_step)
    grads = launch(
        last_kernel, "last", 5, [row(D, BF16)] * 4, main_slots(3), [place, info],
        [res0, dq0, own0, recv0, ig1, ig2, ig3], ([w_down], sources),
    )
    terms, got, *grads = tied((terms, got, *grads))
    terms = terms + got
    moved = [flip(grads[bits], "section", bits) for bits in (1, 2, 3)]
    for axis, bit in (*middle_steps, last_step):
        terms = terms + flip(terms, axis, bit)
    terms, *moved = tied((terms, *moved))
    hidden_states = spread(*outputs, section, core)
    input_grads = spread(grads[0], *moved, section, core)
    grad_main = terms[:, :8].reshape(4, FF)
    return (hidden_states, input_grads, grad_main, terms[:, 8:])


def solution(mesh):
    placed = (
        P(None, "dp", None, None),
        P(None, "dp"),
        P("section", None, None),
        P(),
        P("section", None),
        P("section", None),
        P(),
        P(None, "dp", None, None),
    )
    return jax.shard_map(
        per_device,
        mesh=mesh,
        in_specs=placed,
        out_specs=(
            P("section", None, "dp", None, None),
            P("section", None, "dp", None, None),
            P(),
            P(),
        ),
        check_vma=False,
    )
```

```python
import functools

import jax
import jax.numpy as jnp
from jax import lax
from jax.experimental import pallas as pl
from jax.experimental.pallas import tpu as pltpu
from jax.sharding import PartitionSpec as P

D = 1024
HEADS = 16
HEAD = 64
FF = 4096
EPSILON = 1e-12
NEGATIVE = -1e30
EXTRA = 16

F32, BF16 = (jnp.float32, jnp.bfloat16)
NN = (((1,), (0,)), ((), ()))
NT = (((1,), (1,)), ((), ()))
TN = (((0,), (0,)), ((), ()))
IN_VMEM = pl.BlockSpec(memory_space=pltpu.VMEM)
IN_SMEM = pl.BlockSpec(memory_space=pltpu.SMEM)
IN_HBM = pl.BlockSpec(memory_space=pl.ANY)
SHAPE = jax.ShapeDtypeStruct


def dot(left, right, dims=NN):
    return lax.dot_general(left, right, dims, preferred_element_type=F32)


ONE, TWO, MIDDLE = (448, 576, 256)
LATE = TWO - MIDDLE
PIECES = (
    ((1, 0, 0, ONE), (2, EXTRA, ONE, TWO)),
    ((3, 0, 0, ONE), (4, 0, ONE, TWO)),
    ((5, 0, 0, ONE), (6, EXTRA, ONE, TWO)),
    ((6, EXTRA + TWO, 0, ONE), (7, 0, ONE, TWO)),
    ((8, 0, 0, ONE), (9, EXTRA, ONE, TWO)),
    ((10, 0, 0, ONE + MIDDLE), (9, EXTRA + TWO, ONE + MIDDLE, LATE)),
    ((5, ONE, 0, ONE), (11, EXTRA, ONE, TWO)),
    ((12, 0, 0, ONE + MIDDLE), (11, EXTRA + TWO, ONE + MIDDLE, LATE)),
    ((13, 0, 0, ONE), (14, EXTRA, ONE, TWO)),
    ((15, 0, 0, ONE), (16, 0, ONE, TWO)),
    ((17, 0, 0, ONE), (18, EXTRA, ONE, TWO)),
    ((19, 0, 0, ONE), (20, 0, ONE, TWO)),
)


def fetch_main(place, row, sources, blocks, kept, sems):
    for slot, block in blocks:

        @pl.when(place[row, block] == 0)
        def _():
            pltpu.make_async_copy(
                sources[0].at[:, pl.ds(block * D, D)], kept.at[slot], sems.at[slot]
            ).start()

        for which, pieces in enumerate(PIECES):

            @pl.when(place[row, block] == 1 + which)
            def _():
                for source, at, to, rows in pieces:
                    pltpu.make_async_copy(
                        sources[source].at[pl.ds(at, rows), :],
                        kept.at[slot, pl.ds(to, rows), :],
                        sems.at[slot],
                    ).start()


def fetch_down(w_down, layer, block, kept, slot, sems):
    pltpu.make_async_copy(
        w_down.at[layer, pl.ds(block * D, D), :], kept.at[slot], sems.at[slot]
    ).start()


def wait_slot(w_down, kept, slot, sems):
    pltpu.make_async_copy(w_down.at[0, pl.ds(0, D), :], kept.at[slot], sems.at[slot]).wait()


def norm_forward(residual, gain, shift):
    center = residual - jnp.mean(residual, axis=1, keepdims=True)
    scale = lax.rsqrt(jnp.mean(center * center, axis=1, keepdims=True) + EPSILON)
    normed = center * scale
    return ((normed * gain + shift).astype(BF16), normed.astype(BF16), scale)


def norm_backward(grad, normed, scale, gain):
    up = grad * gain
    first = jnp.mean(up, axis=1, keepdims=True)
    second = jnp.mean(up * normed, axis=1, keepdims=True)
    return (up - first - normed * second) * scale


def lane_halves():
    lane = lax.broadcasted_iota(jnp.int32, (1, 128), 1)
    return (lane < HEAD, lane >= HEAD)


def project(hidden, biases, kept, slots, q_out, kv_out, wait):
    wait(slots[0])
    queries = (dot(hidden, kept[slots[0]]) + biases[:, :D]).astype(BF16)
    q_out[...] = queries * BF16(HEAD ** (-0.5))
    wait(slots[1])
    kv_out[:, :D] = dot(hidden, kept[slots[1]]).astype(BF16)
    wait(slots[2])
    kv_out[:, D:] = (dot(hidden, kept[slots[2]]) + biases[:, D : 2 * D]).astype(BF16)


def attend(q_ref, kv, length, attended, log_out, step):
    rows, keys = (q_ref.shape[0], kv.shape[0])
    position = lax.broadcasted_iota(jnp.int32, (1, keys), 1)
    mask = jnp.where(position < length, 0.0, NEGATIVE).astype(F32)
    halves = lane_halves()
    lane = lax.broadcasted_iota(jnp.int32, (1, 128), 1)
    tops = jnp.zeros((rows, 128), F32)
    sums = jnp.ones((rows, 128), F32)
    for pair in range(HEADS // 2):
        step()
        at = slice(pair * 128, pair * 128 + 128)
        keys_pair, values_pair, queries = (kv[:, at], kv[:, D + at.start : D + at.stop], q_ref[:, at])
        parts = []
        for which in range(2):
            mine = halves[which]
            scores = dot(jnp.where(mine, queries, BF16(0)), keys_pair, NT) + mask
            top = jnp.max(scores, axis=1, keepdims=True)
            powers = jnp.exp(scores - top).astype(BF16)
            both = dot(powers, jnp.where(mine, values_pair, BF16(1)))
            parts.append(both * (1.0 / pltpu.roll(both, HEAD, 1)))
            place = lane == (HEAD * (1 - which) + pair)
            tops = jnp.where(place, top, tops)
            sums = jnp.where(place, both, sums)
        attended[:, at] = jnp.where(halves[0], parts[0], parts[1]).astype(BF16)
    log_out[...] = (tops + jnp.log(sums)).T


def attend_backward(grad_att, q_ref, kv, log_ref, mask, dq_out, dkv):
    halves = lane_halves()
    for pair in range(HEADS // 2):
        at = slice(pair * 128, pair * 128 + 128)
        low = slice(D + at.start, D + at.stop)
        keys_pair, values_pair, queries, grads = (kv[:, at], kv[:, low], q_ref[:, at], grad_att[:, at])
        grad_q = grad_k = grad_v = None
        for which in range(2):
            mine = halves[which]
            q_mine = jnp.where(mine, queries, BF16(0))
            g_mine = jnp.where(mine, grads, BF16(0))
            row = HEAD * (1 - which) + pair
            scores = dot(keys_pair, q_mine, NT) + mask[...]
            soft = jnp.exp(scores - log_ref[row : row + 1, :])
            grad_soft = dot(values_pair, g_mine, NT)
            total = jnp.sum(soft * grad_soft, axis=0, keepdims=True)
            grad_scores = (soft * (grad_soft - total)).astype(BF16)
            part_v = dot(soft.astype(BF16), g_mine)
            part_k = dot(grad_scores, q_mine)
            part_q = dot(grad_scores, jnp.where(mine, keys_pair, BF16(0)), TN)
            grad_v = part_v if which == 0 else grad_v + part_v
            grad_k = part_k if which == 0 else grad_k + part_k
            grad_q = part_q if which == 0 else grad_q + part_q
        dq_out[:, at] = grad_q * HEAD ** (-0.5)
        dkv[:, at] = grad_k
        dkv[:, low] = grad_v


def gelu_pair(value):
    below = 0.5 + 0.5 * lax.erf(value * 0.7071067811865476)
    return (value * below, below + value * (0.3989422804014327 * jnp.exp(value * value * -0.5)))


def feed_forward(hidden, biases, first_slots, second_slots, kept, act, slope, wait, step):
    total = None
    for block in range(4):
        step()
        wait(first_slots[block])
        full = slice(block * D, block * D + D)
        value, grad = gelu_pair(dot(hidden, kept[first_slots[block]]) + biases[:, full])
        slope[:, full] = grad.astype(BF16)
        act[:, full] = value.astype(BF16)
        wait(second_slots[block])
        part = dot(act[:, full], kept[second_slots[block]])
        total = part if total is None else total + part
    return total


def feed_backward(grad_low, slope, first_slots, second_slots, kept, act, terms, wait, step):
    total = None
    for block in range(4):
        step()
        full = slice(block * D, block * D + D)
        wait(second_slots[block])
        grad = dot(grad_low, kept[second_slots[block]], NT) * slope[:, full].astype(F32)
        terms[4 + block : 5 + block, :] = jnp.sum(grad, axis=0, keepdims=True)
        act[:, full] = grad.astype(BF16)
        wait(first_slots[block])
        part = dot(act[:, full], kept[first_slots[block]], NT)
        total = part if total is None else total + part
    return total


def gather_keys(kv_own, kv_other, half, kv, sems):
    rows = kv_own.shape[0]
    mine = pltpu.make_async_copy(kv_own, kv.at[pl.ds(pl.multiple_of(half * rows, rows), rows), :], sems.at[0])
    other = pltpu.make_async_copy(
        kv_other, kv.at[pl.ds(pl.multiple_of((1 - half) * rows, rows), rows), :], sems.at[1]
    )
    return (mine, other)


class Loads:
    def __init__(self, place, sources, w_down, kept, sems):
        self.place, self.sources, self.w_down, self.kept, self.sems = (place, sources, w_down, kept, sems)
        self.starts = []

    def main(self, section, *slots):
        for slot, block in slots:
            self.starts.append(
                lambda slot=slot, block=block: fetch_main(
                    self.place, section, self.sources, ((slot, block),), self.kept, self.sems
                )
            )

    def down(self, layer, slot, block):
        self.starts.append(lambda: fetch_down(self.w_down, layer, block, self.kept, slot, self.sems))

    def copies(self, *copies):
        self.starts.append(lambda: [copy.start() for copy in copies])

    def step(self, count=1):
        for _ in range(count):
            if self.starts:
                self.starts.pop(0)()

    def wait(self, slot):
        wait_slot(self.w_down, self.kept, slot, self.sems)


def first_kernel(n_main, place, hidden, main_bias, w_down, *refs):
    sources = refs[:n_main]
    q_out, kv_out, kept, sems = refs[n_main:]
    loads = Loads(place, sources, w_down, kept, sems)
    loads.main(0, (0, 0), (1, 1), (2, 2))
    loads.step(3)
    project(hidden[...], main_bias[0:1, :], kept, (0, 1, 2), q_out, kv_out, loads.wait)


def low_kernel(n_main, place, info, hidden, q_in, main_bias, down_bias, gains, kv_own, kv_other, w_down, *refs):
    sources = refs[:n_main]
    (
        mid_out, out_out, q_out, kv_out, log_out, norm_a, scale_a, norm_f, scale_f, slope,
        kept, sems, kv, kv_sems, attended, act,
    ) = refs[n_main:]
    keys = gather_keys(kv_own, kv_other, info[1], kv, kv_sems)
    loads = Loads(place, sources, w_down, kept, sems)
    wait, step = (loads.wait, loads.step)
    loads.copies(*keys)
    loads.main(0, (0, 3))
    for block in range(4):
        loads.main(1, (1 + block, block))
        loads.down(0, 5 + block, block)
    loads.main(2, (9, 0), (10, 1), (11, 2))
    step(2)
    for key in keys:
        key.wait()
    attend(q_in, kv, info[0], attended, log_out, step)
    wait(0)
    residual = hidden[...].astype(F32) + dot(attended[...], kept[0]) + main_bias[0:1, 2 * D : 3 * D]
    mid, norm, scale = norm_forward(residual, gains[0:1, :], main_bias[0:1, 3 * D :])
    mid_out[...] = mid
    norm_a[...] = norm
    scale_a[...] = jnp.broadcast_to(scale, scale_a.shape)
    hidden_now = mid_out[...]
    total = feed_forward(
        hidden_now, main_bias[1:2, :], (1, 2, 3, 4), (5, 6, 7, 8), kept, act, slope, wait, step
    )
    residual = mid_out[...].astype(F32) + total + down_bias[0:1, :]
    out, norm, scale = norm_forward(residual, gains[1:2, :], down_bias[1:2, :])
    out_out[...] = out
    norm_f[...] = norm
    scale_f[...] = jnp.broadcast_to(scale, scale_f.shape)
    project(out_out[...], main_bias[2:3, :], kept, (9, 10, 11), q_out, kv_out, wait)


def start_attention_backward(grad, norm, scale, gain, w_out, grad_res, grad_att, terms):
    grad_float = grad.astype(F32)
    grad_now = norm_backward(grad_float, norm.astype(F32), scale, gain)
    grad_res[...] = grad_now
    terms[2:3, :] = jnp.sum(grad_now, axis=0, keepdims=True)
    terms[3:4, :] = jnp.sum(grad_float, axis=0, keepdims=True)
    grad_att[...] = dot(grad_now.astype(BF16), w_out, NT).astype(BF16)


def finish_attention_backward(half, dq, dkv, dq_out, own_out, other_out, terms):
    rows = dq.shape[0]
    grad_q = dq[...]
    dq_out[...] = grad_q.astype(BF16)
    terms[0:1, :] = jnp.sum(grad_q, axis=0, keepdims=True)
    terms[1:2, :] = jnp.sum(dkv[:, D:], axis=0, keepdims=True)
    own_out[...] = dkv[pl.ds(pl.multiple_of(half * rows, rows), rows), :].astype(BF16)
    other_out[...] = dkv[pl.ds(pl.multiple_of((1 - half) * rows, rows), rows), :].astype(BF16)


def fill_mask(mask, length):
    position = lax.broadcasted_iota(jnp.int32, mask.shape, 0)
    mask[...] = jnp.where(position < length, 0.0, NEGATIVE).astype(F32)


def high_kernel(n_main, place, info, hidden, q_in, cotangent, main_bias, down_bias, gains, kv_own, kv_other, w_down, *refs):
    sources = refs[:n_main]
    (
        mid_out, out_out, ig_out, dq_out, own_out, other_out, grad_res, terms,
        kept, sems, kv, kv_sems, attended, act, slope, mask, logs, norm_a, dq, dkv,
    ) = refs[n_main:]
    keys = gather_keys(kv_own, kv_other, info[1], kv, kv_sems)
    loads = Loads(place, sources, w_down, kept, sems)
    wait, step = (loads.wait, loads.step)
    loads.copies(*keys)
    loads.main(2, (0, 3))
    for block in range(4):
        loads.main(3, (1 + block, block))
        loads.down(1, 5 + block, block)
    done = lambda slot: None
    step(2)
    fill_mask(mask, info[0])
    for key in keys:
        key.wait()
    attend(q_in, kv, info[0], attended, logs, step)
    wait(0)
    residual = hidden[...].astype(F32) + dot(attended[...], kept[0]) + main_bias[2:3, 2 * D : 3 * D]
    mid, norm, scale_mid = norm_forward(residual, gains[2:3, :], main_bias[2:3, 3 * D :])
    mid_out[...] = mid
    norm_a[...] = norm
    hidden_now = mid_out[...]
    total = feed_forward(
        hidden_now, main_bias[3:4, :], (1, 2, 3, 4), (5, 6, 7, 8), kept, act, slope, wait, step
    )
    residual = mid_out[...].astype(F32) + total + down_bias[2:3, :]
    out, norm, scale = norm_forward(residual, gains[3:4, :], down_bias[3:4, :])
    out_out[...] = out
    grad_float = cotangent[...].astype(F32)
    grad_now = norm_backward(grad_float, norm.astype(F32), scale, gains[3:4, :])
    terms[8:9, :] = jnp.sum(grad_now, axis=0, keepdims=True)
    terms[9:10, :] = jnp.sum(grad_float, axis=0, keepdims=True)
    total = feed_backward(
        grad_now.astype(BF16), slope, (1, 2, 3, 4), (5, 6, 7, 8), kept, act, terms, done, step
    )
    ig_out[...] = (grad_now + total).astype(BF16)
    start_attention_backward(
        ig_out[...], norm_a[...], scale_mid, gains[2:3, :], kept[0], grad_res, attended, terms
    )
    attend_backward(attended, q_in, kv, logs, mask, dq, dkv)
    finish_attention_backward(info[1], dq, dkv, dq_out, own_out, other_out, terms)


def input_grad(grad_res, dq_in, own_in, recv_in, kept, slots, wait, step):
    wait(slots[0])
    step()
    total = grad_res[...] + dot(dq_in[...], kept[slots[0]], NT)
    grads = (own_in[...].astype(F32) + recv_in[...].astype(F32)).astype(BF16)
    wait(slots[1])
    step()
    total = total + dot(grads[:, :D], kept[slots[1]], NT)
    wait(slots[2])
    step()
    return (total + dot(grads[:, D:], kept[slots[2]], NT)).astype(BF16)


def back_kernel(
    n_main, place, info, grad_in, dq_in, own_in, recv_in, gains, scale_f, scale_a, logs, high_terms, norm_f, slope,
    norm_a, q_in, kv_own, kv_other, w_down, *refs
):
    sources = refs[:n_main]
    (
        ig_high, ig_out, dq_out, own_out, other_out, grad_res, all_terms,
        kept, sems, kv, kv_sems, grad_att, act, mask, dq, dkv, slope_in, rows_in, row_sems,
    ) = refs[n_main:]
    keys = gather_keys(kv_own, kv_other, info[1], kv, kv_sems)
    terms = all_terms.at[0]
    all_terms[1] = high_terms[...]
    slope_copy = pltpu.make_async_copy(slope, slope_in, row_sems.at[3])
    copies = [
        pltpu.make_async_copy(array, rows_in.at[i], row_sems.at[i])
        for i, array in enumerate((norm_f, norm_a, q_in))
    ]
    loads = Loads(place, sources, w_down, kept, sems)
    wait, step = (loads.wait, loads.step)
    loads.main(2, (9, 0), (10, 1), (11, 2))
    loads.copies(copies[0], slope_copy)
    loads.down(0, 5, 0)
    loads.main(1, (1, 0))
    for block in (1, 2, 3):
        loads.down(0, 5 + block, block)
        loads.main(1, (1 + block, block))
    loads.main(0, (0, 3))
    loads.copies(*keys, *copies[1:])
    step(3)
    fill_mask(mask, info[0])
    step()
    ig_high[...] = input_grad(grad_in, dq_in, own_in, recv_in, kept, (9, 10, 11), wait, step)
    grad_float = ig_high[...].astype(F32)
    copies[0].wait()
    grad_now = norm_backward(grad_float, rows_in[0].astype(F32), scale_f[:, 0:1], gains[1:2, :])
    terms[8:9, :] = jnp.sum(grad_now, axis=0, keepdims=True)
    terms[9:10, :] = jnp.sum(grad_float, axis=0, keepdims=True)
    slope_copy.wait()
    total = feed_backward(
        grad_now.astype(BF16), slope_in, (1, 2, 3, 4), (5, 6, 7, 8), kept, act, terms, wait, lambda: step(2)
    )
    ig_out[...] = (grad_now + total).astype(BF16)
    step(8)
    wait(0)
    for copy in (*keys, *copies[1:]):
        copy.wait()
    start_attention_backward(
        ig_out[...], rows_in[1], scale_a[:, 0:1], gains[0:1, :], kept[0], grad_res, grad_att, terms
    )
    attend_backward(grad_att, rows_in.at[2], kv, logs, mask, dq, dkv)
    finish_attention_backward(info[1], dq, dkv, dq_out, own_out, other_out, terms)


def last_kernel(n_main, place, info, grad_res, dq_in, own_in, recv_in, ig_one, ig_two, ig_three, w_down, *refs):
    sources = refs[:n_main]
    *outs, kept, sems = refs[n_main:]
    loads = Loads(place, sources, w_down, kept, sems)
    loads.main(0, (0, 0), (1, 1), (2, 2))
    loads.step(3)
    for section, grads in ((1, ig_one), (2, ig_two), (3, ig_three)):
        for bits, out in enumerate(outs):

            @pl.when(info[2] == section ^ bits)
            def _():
                out[...] = grads[...]

    grads = input_grad(grad_res, dq_in, own_in, recv_in, kept, (0, 1, 2), loads.wait, loads.step)
    for bits, out in enumerate(outs):

        @pl.when(info[2] == bits)
        def _():
            out[...] = grads


def launch(kernel, name, work, outs, scratch, smem, vmem, hbm):
    return pl.pallas_call(
        functools.partial(kernel, len(hbm[1])),
        name=name,
        out_shape=outs,
        in_specs=[IN_SMEM] * len(smem)
        + [IN_VMEM] * len(vmem)
        + [IN_HBM] * (len(hbm[0]) + len(hbm[1])),
        out_specs=[IN_VMEM] * len(outs),
        scratch_shapes=scratch,
        cost_estimate=pl.CostEstimate(flops=int(work * 1e9), bytes_accessed=2**20, transcendentals=0),
        compiler_params=pltpu.CompilerParams(vmem_limit_bytes=58 * 2**20),
    )(*smem, *vmem, *hbm[0], *hbm[1])


def main_slots(count):
    return [pltpu.VMEM((count, D, D), BF16), pltpu.SemaphoreType.DMA((count,))]


def flip(value, axis, bit):
    count = lax.axis_size(axis)
    return lax.ppermute(value, axis, [(source, source ^ bit) for source in range(count)])


def tied(value, *others):
    return lax.optimization_barrier((value, *others))[0]


def split_three(value):
    high = lax.optimization_barrier(value.astype(BF16))
    rest = value - high.astype(F32)
    middle = lax.optimization_barrier(rest.astype(BF16))
    low = (rest - middle.astype(F32)).astype(BF16)
    return jnp.concatenate([high.reshape(-1, D), middle.reshape(-1, D), low.reshape(-1, D)])


def join_three(rows):
    parts = rows.astype(F32).reshape(3, -1)
    return parts[0] + parts[1] + parts[2]


def tied(values, *others):
    return lax.optimization_barrier((*values, *others))[: len(values)]


def gather_weights(own, base, small, early, finish):
    over_x = lambda value: flip(value, "section", 1)
    over_y = lambda value: flip(value, "section", 2)
    over_z = lambda value: flip(value, "dp", 2)
    over_core = lambda value: flip(value, "dp", 1)
    first = lax.dynamic_slice(own, (0, base * D), (ONE, D))
    second = lax.dynamic_slice(own, (ONE - EXTRA, base * D), (EXTRA + TWO, D))
    extra = split_three(small)
    rows = extra.shape[0]
    second = lax.dynamic_update_slice(lax.optimization_barrier(second), extra, (0, 0))
    far = lax.dynamic_slice(own, (ONE + MIDDLE, (base ^ 1) * D), (LATE, D))
    x_one, y_one, x_two = (over_x(first), over_y(first), over_x(second))
    y_two = over_y(jnp.concatenate([second, far]))
    early = early(first)

    x_first, y_first = tied((x_one, y_one))
    xz_one, d_one = (over_z(x_first), over_x(y_first))
    ones = jnp.concatenate([x_first, y_first])

    x_second, z_now, ones = tied((x_two, xz_one, ones), *early)
    dz_one, xz_two, c_ones = (over_y(z_now), over_z(x_second[EXTRA:]), over_core(ones))
    mixed = jnp.concatenate([x_second, z_now])

    y_second = y_two
    rest = jnp.concatenate([y_first, y_second[EXTRA : EXTRA + MIDDLE]])
    d_now, dz_now, xz_now, y_second, rest, mixed = tied((d_one, dz_one, xz_two, y_second, rest, mixed), c_ones)
    dz_two, yz, d_two = (over_y(xz_now), over_z(rest), over_x(y_second[: EXTRA + TWO]))
    c_mixed, yc_two = (over_core(mixed), over_core(y_second))

    two_now, dz_last, z_now, d_now, dz_now, xz_now = tied(
        (d_two, dz_two, yz, d_now, dz_now, xz_now), c_mixed, yc_two
    )
    dc_one, dzc_one, xzc_two = (over_core(d_now), over_core(dz_now), over_core(xz_now))
    dc_two, dzc_two, yzc = (over_core(two_now), over_core(dz_last), over_core(z_now))
    smalls = jnp.stack([small] + [join_three(piece[:rows]) for piece in (x_two, y_two, two_now)])
    smalls = finish(smalls)
    received = (
        x_one, x_two, xz_one, xz_two, c_ones, c_mixed, xzc_two, y_one, y_two, yz, yc_two, yzc,
        d_one, d_two, dz_one, dz_two, dc_one, dc_two, dzc_one, dzc_two,
    )
    return (list(received), smalls, early)


def butterfly_steps():
    steps = {}
    for axis in ("dp", "section"):
        bits = []
        while 2 ** len(bits) < lax.axis_size(axis):
            bits.append(2 ** len(bits))
        steps[axis] = [(axis, bit) for bit in bits]
    return steps["dp"][:1] + steps["section"][:1] + steps["dp"][1:] + steps["section"][1:]


def choose(values, index):
    low = jnp.where(index % 2 == 0, values[0], values[1])
    high = jnp.where(index % 2 == 0, values[2], values[3])
    return jnp.where(index < 2, low, high)


def pick(stack, index):
    return lax.dynamic_index_in_dim(stack, index, 0, keepdims=False)


def spread(mine, got_x, got_y, got_d, section, core):
    same = core == section % 2
    keep_first = jnp.where(same, mine, got_x)
    keep_second = jnp.where(same, got_y, got_d)
    send = jnp.stack([jnp.where(same, got_x, mine), jnp.where(same, got_d, got_y)])
    got = flip(send, "dp", 1)
    batch = section // 2
    kept_rows = [jnp.where(batch == 0, keep_first, keep_second), jnp.where(batch == 0, keep_second, keep_first)]
    got_rows = [jnp.where(batch == 0, got[0], got[1]), jnp.where(batch == 0, got[1], got[0])]
    parts = []
    for kept_now, got_now in zip(kept_rows, got_rows):
        parts.append(
            jnp.concatenate(
                [jnp.where(core == 0, kept_now, got_now), jnp.where(core == 0, got_now, kept_now)]
            )
        )
    return jnp.stack(parts)[None, :, None]


def per_device(inputs_x, lengths, w_main, w_down, gains, bias_main, bias_down, cotangent):
    section = lax.axis_index("section")
    lane = lax.axis_index("dp")
    core, plane = (lane % 2, (lane // 2) % 2)
    base = core * 2 + plane
    rows = inputs_x.shape[2] // 2

    batch = section // 2
    same = core == section % 2
    blocks = jnp.arange(4, dtype=jnp.int32)[None, :]
    away = section ^ jnp.arange(4, dtype=jnp.int32)[:, None]

    def take_inputs(after):
        tied_x, tied_grad, tied_lengths, _ = lax.optimization_barrier((inputs_x, cotangent, lengths, after))
        lines = jnp.stack([pick(tied_x[:, 0], batch), pick(tied_grad[:, 0], batch)])
        mine = lax.dynamic_slice_in_dim(lines, core * rows, rows, axis=1)
        other = flip(lax.dynamic_slice_in_dim(lines, (1 - core) * rows, rows, axis=1), "dp", 1)
        mine = jnp.where(same, mine, other)
        length_own = lax.dynamic_slice_in_dim(tied_lengths[:, 0], batch, 1).astype(F32)
        length_other = flip(jnp.broadcast_to(length_own[None], (8, 128)), "dp", 1)[0, :1]
        length = jnp.where(same, length_own, length_other).astype(jnp.int32)
        info = jnp.concatenate([length, core[None].astype(jnp.int32), section[None].astype(jnp.int32)])
        place = jnp.where(away == 0, 0, 1 + (away - 1) * 4 + (blocks ^ base)).astype(jnp.int32)
        return (mine[0], mine[1], info, place)

    small = jnp.concatenate([gains, bias_main], axis=1).reshape(-1)
    own = w_main[0]

    def take_smalls(smalls):
        smalls = jnp.stack([pick(smalls, section ^ s) for s in range(4)])
        return (smalls[:, :D], smalls[:, D:], bias_down.reshape(4, D))

    received, smalls, early = gather_weights(own, base, small, take_inputs, take_smalls)
    hidden, grad_last, info, place = early
    all_gains, all_bias, down_bias = smalls
    sources = [own] + received

    def row(width, kind):
        return SHAPE((rows, width), kind)

    pair_sems = pltpu.SemaphoreType.DMA((2,))
    keys = pltpu.VMEM((2 * rows, 2 * D), BF16)
    q0, kv0 = launch(
        first_kernel, "first", 5, [row(D, BF16), row(2 * D, BF16)], main_slots(3),
        [place], [hidden, all_bias], ([w_down], sources),
    )
    kv0_other = flip(kv0, "dp", 1)
    hs0, hs1, q2, kv2, logs0, norm0, scale0, norm1, scale1, slope1 = launch(
        low_kernel, "low", 20,
        [
            row(D, BF16), row(D, BF16), row(D, BF16), row(2 * D, BF16), SHAPE((128, rows), F32),
            row(D, BF16), row(128, F32), row(D, BF16), row(128, F32), row(FF, BF16),
        ],
        main_slots(12)
        + [keys, pair_sems, pltpu.VMEM((rows, D), BF16), pltpu.VMEM((rows, FF), BF16)],
        [place, info], [hidden, q0, all_bias, down_bias, all_gains, kv0, kv0_other], ([w_down], sources),
    )
    kv2_other = flip(kv2, "dp", 1)
    hs2, hs3, ig3, dq2, own2, other2, res2, terms2 = launch(
        high_kernel, "high", 32,
        [
            row(D, BF16), row(D, BF16), row(D, BF16), row(D, BF16), row(2 * D, BF16), row(2 * D, BF16),
            row(D, F32), SHAPE((10, D), F32),
        ],
        main_slots(9)
        + [
            keys, pair_sems, pltpu.VMEM((rows, D), BF16), pltpu.VMEM((rows, FF), BF16),
            pltpu.VMEM((rows, FF), BF16), pltpu.VMEM((2 * rows, rows), F32), pltpu.VMEM((128, rows), F32),
            pltpu.VMEM((rows, D), BF16), pltpu.VMEM((rows, D), F32), pltpu.VMEM((2 * rows, 2 * D), F32),
        ],
        [place, info], [hs1, q2, grad_last, all_bias, down_bias, all_gains, kv2, kv2_other],
        ([w_down], sources),
    )
    recv2 = flip(other2, "dp", 1)
    ig2, ig1, dq0, own0, other0, res0, terms = launch(
        back_kernel, "back", 20,
        [
            row(D, BF16), row(D, BF16), row(D, BF16), row(2 * D, BF16), row(2 * D, BF16), row(D, F32),
            SHAPE((2, 10, D), F32),
        ],
        main_slots(12)
        + [
            keys, pair_sems, pltpu.VMEM((rows, D), BF16), pltpu.VMEM((rows, FF), BF16),
            pltpu.VMEM((2 * rows, rows), F32), pltpu.VMEM((rows, D), F32), pltpu.VMEM((2 * rows, 2 * D), F32),
            pltpu.VMEM((rows, FF), BF16), pltpu.VMEM((3, rows, D), BF16), pltpu.SemaphoreType.DMA((4,)),
        ],
        [place, info],
        [res2, dq2, own2, recv2, all_gains, scale1, scale0, logs0, terms2],
        ([norm1, slope1, norm0, q0, kv0, kv0_other, w_down], sources),
    )
    outputs = [choose((hs0, hs1, hs2, hs3), section ^ bits) for bits in range(4)]
    outputs = [outputs[0]] + [flip(outputs[bits], "section", bits) for bits in (1, 2, 3)]
    other0, terms, res0, *outputs = tied((other0, terms, res0, *outputs))
    recv0 = flip(other0, "dp", 1)
    core_step, first_step, *middle_steps = butterfly_steps()
    terms = terms + flip(terms, *core_step)
    got = flip(terms, *first_step)
    grads = launch(
        last_kernel, "last", 5, [row(D, BF16)] * 4, main_slots(3), [place, info],
        [res0, dq0, own0, recv0, ig1, ig2, ig3], ([w_down], sources),
    )
    terms, got, *grads = tied((terms, got, *grads))
    terms = terms + got
    moved = [flip(grads[bits], "section", bits) for bits in (1, 2, 3)]
    for axis, bit in middle_steps:
        terms = terms + flip(terms, axis, bit)
    terms, *moved = tied((terms, *moved))
    hidden_states = spread(*outputs, section, core)
    input_grads = spread(grads[0], *moved, section, core)
    grad_main = terms[:, :8].reshape(4, FF)
    return (hidden_states, input_grads, grad_main, terms[:, 8:])


def solution(mesh):
    placed = (
        P(None, "dp", None, None),
        P(None, "dp"),
        P("section", None, None),
        P(),
        P("section", None),
        P("section", None),
        P(),
        P(None, "dp", None, None),
    )
    return jax.shard_map(
        per_device,
        mesh=mesh,
        in_specs=placed,
        out_specs=(
            P("section", None, "dp", None, None),
            P("section", None, "dp", None, None),
            P(),
            P(),
        ),
        check_vma=False,
    )
```

```python
import functools

import jax
import jax.numpy as jnp
from jax import lax
from jax.experimental import pallas as pl
from jax.experimental.pallas import tpu as pltpu
from jax.sharding import PartitionSpec as P

D = 1024
HEADS = 16
HEAD = 64
FF = 4096
EPSILON = 1e-12
NEGATIVE = -1e30
EXTRA = 16

F32, BF16 = (jnp.float32, jnp.bfloat16)
NN = (((1,), (0,)), ((), ()))
NT = (((1,), (1,)), ((), ()))
TN = (((0,), (0,)), ((), ()))
IN_VMEM = pl.BlockSpec(memory_space=pltpu.VMEM)
IN_SMEM = pl.BlockSpec(memory_space=pltpu.SMEM)
IN_HBM = pl.BlockSpec(memory_space=pl.ANY)
SHAPE = jax.ShapeDtypeStruct


def dot(left, right, dims=NN):
    return lax.dot_general(left, right, dims, preferred_element_type=F32)


ONE, TWO, MIDDLE = (448, 576, 256)
LATE = TWO - MIDDLE
PIECES = (
    ((1, 0, 0, ONE), (2, EXTRA, ONE, TWO)),
    ((3, 0, 0, ONE), (4, 0, ONE, TWO)),
    ((5, 0, 0, ONE), (6, EXTRA, ONE, TWO)),
    ((6, EXTRA + TWO, 0, ONE), (7, 0, ONE, TWO)),
    ((8, 0, 0, ONE), (9, EXTRA, ONE, TWO)),
    ((10, 0, 0, ONE + MIDDLE), (9, EXTRA + TWO, ONE + MIDDLE, LATE)),
    ((5, ONE, 0, ONE), (11, EXTRA, ONE, TWO)),
    ((12, 0, 0, ONE + MIDDLE), (11, EXTRA + TWO, ONE + MIDDLE, LATE)),
    ((13, 0, 0, ONE), (14, EXTRA, ONE, TWO)),
    ((15, 0, 0, ONE), (16, 0, ONE, TWO)),
    ((17, 0, 0, ONE), (18, EXTRA, ONE, TWO)),
    ((19, 0, 0, ONE), (20, 0, ONE, TWO)),
)


def fetch_main(place, row, sources, blocks, kept, sems):
    for slot, block in blocks:

        @pl.when(place[row, block] == 0)
        def _():
            pltpu.make_async_copy(
                sources[0].at[:, pl.ds(block * D, D)], kept.at[slot], sems.at[slot]
            ).start()

        for which, pieces in enumerate(PIECES):

            @pl.when(place[row, block] == 1 + which)
            def _():
                for source, at, to, rows in pieces:
                    pltpu.make_async_copy(
                        sources[source].at[pl.ds(at, rows), :],
                        kept.at[slot, pl.ds(to, rows), :],
                        sems.at[slot],
                    ).start()


def fetch_down(w_down, layer, block, kept, slot, sems):
    pltpu.make_async_copy(
        w_down.at[layer, pl.ds(block * D, D), :], kept.at[slot], sems.at[slot]
    ).start()


def wait_slot(w_down, kept, slot, sems):
    pltpu.make_async_copy(w_down.at[0, pl.ds(0, D), :], kept.at[slot], sems.at[slot]).wait()


def norm_forward(residual, gain, shift):
    center = residual - jnp.mean(residual, axis=1, keepdims=True)
    scale = lax.rsqrt(jnp.mean(center * center, axis=1, keepdims=True) + EPSILON)
    normed = center * scale
    return ((normed * gain + shift).astype(BF16), normed.astype(BF16), scale)


def norm_backward(grad, normed, scale, gain):
    up = grad * gain
    first = jnp.mean(up, axis=1, keepdims=True)
    second = jnp.mean(up * normed, axis=1, keepdims=True)
    return (up - first - normed * second) * scale


def lane_halves():
    lane = lax.broadcasted_iota(jnp.int32, (1, 128), 1)
    return (lane < HEAD, lane >= HEAD)


def project(hidden, biases, kept, slots, q_out, kv_out, wait):
    wait(slots[0])
    queries = (dot(hidden, kept[slots[0]]) + biases[:, :D]).astype(BF16)
    q_out[...] = queries * BF16(HEAD ** (-0.5))
    wait(slots[1])
    kv_out[:, :D] = dot(hidden, kept[slots[1]]).astype(BF16)
    wait(slots[2])
    kv_out[:, D:] = (dot(hidden, kept[slots[2]]) + biases[:, D : 2 * D]).astype(BF16)


def two_heads(pair_columns):
    halves = lane_halves()
    return jnp.concatenate([jnp.where(mine, pair_columns, BF16(0)) for mine in halves])


def attend(q_ref, kv, length, attended, log_out, step):
    rows, keys = (q_ref.shape[0], kv.shape[0])
    position = lax.broadcasted_iota(jnp.int32, (1, keys), 1)
    mask = jnp.where(position < length, 0.0, NEGATIVE).astype(F32)
    halves = lane_halves()
    lane = lax.broadcasted_iota(jnp.int32, (1, 128), 1)
    ones = jnp.ones((keys, 128), BF16)
    tops = jnp.zeros((rows, 128), F32)
    sums = jnp.ones((rows, 128), F32)
    for pair in range(HEADS // 2):
        step()
        at = slice(pair * 128, pair * 128 + 128)
        keys_pair, values_pair = (kv[:, at], kv[:, D + at.start : D + at.stop])
        scores = dot(two_heads(q_ref[:, at]), keys_pair, NT) + mask
        top = jnp.max(scores, axis=1, keepdims=True)
        powers = jnp.exp(scores - top).astype(BF16)
        both = dot(powers, jnp.concatenate([values_pair, ones], axis=1))
        parts = both[:, :128] * (1.0 / both[:, 128:])
        attended[:, at] = jnp.where(halves[0], parts[:rows], parts[rows:]).astype(BF16)
        for which in range(2):
            mine = slice(which * rows, which * rows + rows)
            place = lane == (HEAD * (1 - which) + pair)
            tops = jnp.where(place, top[mine], tops)
            sums = jnp.where(place, both[mine, 128:], sums)
    log_out[...] = (tops + jnp.log(sums)).T


def attend_backward(grad_att, q_ref, kv, log_ref, mask, dq_out, dkv):
    halves = lane_halves()
    rows = q_ref.shape[0]
    for pair in range(HEADS // 2):
        at = slice(pair * 128, pair * 128 + 128)
        low = slice(D + at.start, D + at.stop)
        keys_pair, values_pair = (kv[:, at], kv[:, low])
        queries, grads = (two_heads(q_ref[:, at]), two_heads(grad_att[:, at]))
        logs = jnp.concatenate([log_ref[HEAD + pair : HEAD + pair + 1, :], log_ref[pair : pair + 1, :]], axis=1)
        masked = jnp.concatenate([mask[...], mask[...]], axis=1)
        soft = jnp.exp(dot(keys_pair, queries, NT) + masked - logs)
        grad_soft = dot(values_pair, grads, NT)
        total = jnp.sum(soft * grad_soft, axis=0, keepdims=True)
        grad_scores = (soft * (grad_soft - total)).astype(BF16)
        dkv[:, low] = dot(soft.astype(BF16), grads)
        dkv[:, at] = dot(grad_scores, queries)
        grad_q = dot(grad_scores, keys_pair, TN)
        dq_out[:, at] = jnp.where(halves[0], grad_q[:rows], grad_q[rows:]) * HEAD ** (-0.5)


def gelu_pair(value):
    below = 0.5 + 0.5 * lax.erf(value * 0.7071067811865476)
    return (value * below, below + value * (0.3989422804014327 * jnp.exp(value * value * -0.5)))


def feed_forward(hidden, biases, first_slots, second_slots, kept, act, slope, wait, step):
    total = None
    for block in range(4):
        step()
        wait(first_slots[block])
        full = slice(block * D, block * D + D)
        value, grad = gelu_pair(dot(hidden, kept[first_slots[block]]) + biases[:, full])
        slope[:, full] = grad.astype(BF16)
        act[:, full] = value.astype(BF16)
        wait(second_slots[block])
        part = dot(act[:, full], kept[second_slots[block]])
        total = part if total is None else total + part
    return total


def feed_backward(grad_low, slope, first_slots, second_slots, kept, act, terms, wait, step):
    total = None
    for block in range(4):
        step()
        full = slice(block * D, block * D + D)
        wait(second_slots[block])
        grad = dot(grad_low, kept[second_slots[block]], NT) * slope[:, full].astype(F32)
        terms[4 + block : 5 + block, :] = jnp.sum(grad, axis=0, keepdims=True)
        act[:, full] = grad.astype(BF16)
        wait(first_slots[block])
        part = dot(act[:, full], kept[first_slots[block]], NT)
        total = part if total is None else total + part
    return total


def gather_keys(kv_own, kv_other, half, kv, sems):
    rows = kv_own.shape[0]
    mine = pltpu.make_async_copy(kv_own, kv.at[pl.ds(pl.multiple_of(half * rows, rows), rows), :], sems.at[0])
    other = pltpu.make_async_copy(
        kv_other, kv.at[pl.ds(pl.multiple_of((1 - half) * rows, rows), rows), :], sems.at[1]
    )
    return (mine, other)


class Loads:
    def __init__(self, place, sources, w_down, kept, sems):
        self.place, self.sources, self.w_down, self.kept, self.sems = (place, sources, w_down, kept, sems)
        self.starts = []

    def main(self, section, *slots):
        for slot, block in slots:
            self.starts.append(
                lambda slot=slot, block=block: fetch_main(
                    self.place, section, self.sources, ((slot, block),), self.kept, self.sems
                )
            )

    def down(self, layer, slot, block):
        self.starts.append(lambda: fetch_down(self.w_down, layer, block, self.kept, slot, self.sems))

    def copies(self, *copies):
        self.starts.append(lambda: [copy.start() for copy in copies])

    def step(self, count=1):
        for _ in range(count):
            if self.starts:
                self.starts.pop(0)()

    def wait(self, slot):
        wait_slot(self.w_down, self.kept, slot, self.sems)


def first_kernel(n_main, place, hidden, main_bias, w_down, *refs):
    sources = refs[:n_main]
    q_out, kv_out, kept, sems = refs[n_main:]
    loads = Loads(place, sources, w_down, kept, sems)
    loads.main(0, (0, 0), (1, 1), (2, 2))
    loads.step(3)
    project(hidden[...], main_bias[0:1, :], kept, (0, 1, 2), q_out, kv_out, loads.wait)


def low_kernel(n_main, place, info, hidden, q_in, main_bias, down_bias, gains, kv_own, kv_other, w_down, *refs):
    sources = refs[:n_main]
    (
        mid_out, out_out, q_out, kv_out, log_out, norm_a, scale_a, norm_f, scale_f, slope,
        kept, sems, kv, kv_sems, attended, act,
    ) = refs[n_main:]
    keys = gather_keys(kv_own, kv_other, info[1], kv, kv_sems)
    loads = Loads(place, sources, w_down, kept, sems)
    wait, step = (loads.wait, loads.step)
    loads.copies(*keys)
    loads.main(0, (0, 3))
    for block in range(4):
        loads.main(1, (1 + block, block))
        loads.down(0, 5 + block, block)
    loads.main(2, (9, 0), (10, 1), (11, 2))
    step(2)
    for key in keys:
        key.wait()
    attend(q_in, kv, info[0], attended, log_out, step)
    wait(0)
    residual = hidden[...].astype(F32) + dot(attended[...], kept[0]) + main_bias[0:1, 2 * D : 3 * D]
    mid, norm, scale = norm_forward(residual, gains[0:1, :], main_bias[0:1, 3 * D :])
    mid_out[...] = mid
    norm_a[...] = norm
    scale_a[...] = jnp.broadcast_to(scale, scale_a.shape)
    hidden_now = mid_out[...]
    total = feed_forward(
        hidden_now, main_bias[1:2, :], (1, 2, 3, 4), (5, 6, 7, 8), kept, act, slope, wait, step
    )
    residual = mid_out[...].astype(F32) + total + down_bias[0:1, :]
    out, norm, scale = norm_forward(residual, gains[1:2, :], down_bias[1:2, :])
    out_out[...] = out
    norm_f[...] = norm
    scale_f[...] = jnp.broadcast_to(scale, scale_f.shape)
    project(out_out[...], main_bias[2:3, :], kept, (9, 10, 11), q_out, kv_out, wait)


def start_attention_backward(grad, norm, scale, gain, w_out, grad_res, grad_att, terms):
    grad_float = grad.astype(F32)
    grad_now = norm_backward(grad_float, norm.astype(F32), scale, gain)
    grad_res[...] = grad_now
    terms[2:3, :] = jnp.sum(grad_now, axis=0, keepdims=True)
    terms[3:4, :] = jnp.sum(grad_float, axis=0, keepdims=True)
    grad_att[...] = dot(grad_now.astype(BF16), w_out, NT).astype(BF16)


def finish_attention_backward(half, dq, dkv, dq_out, own_out, other_out, terms):
    rows = dq.shape[0]
    grad_q = dq[...]
    dq_out[...] = grad_q.astype(BF16)
    terms[0:1, :] = jnp.sum(grad_q, axis=0, keepdims=True)
    terms[1:2, :] = jnp.sum(dkv[:, D:], axis=0, keepdims=True)
    own_out[...] = dkv[pl.ds(pl.multiple_of(half * rows, rows), rows), :].astype(BF16)
    other_out[...] = dkv[pl.ds(pl.multiple_of((1 - half) * rows, rows), rows), :].astype(BF16)


def fill_mask(mask, length):
    position = lax.broadcasted_iota(jnp.int32, mask.shape, 0)
    mask[...] = jnp.where(position < length, 0.0, NEGATIVE).astype(F32)


def high_kernel(n_main, place, info, hidden, q_in, cotangent, main_bias, down_bias, gains, kv_own, kv_other, w_down, *refs):
    sources = refs[:n_main]
    (
        mid_out, out_out, ig_out, dq_out, own_out, other_out, grad_res, terms,
        kept, sems, kv, kv_sems, attended, act, slope, mask, logs, norm_a, dq, dkv,
    ) = refs[n_main:]
    keys = gather_keys(kv_own, kv_other, info[1], kv, kv_sems)
    loads = Loads(place, sources, w_down, kept, sems)
    wait, step = (loads.wait, loads.step)
    loads.copies(*keys)
    loads.main(2, (0, 3))
    for block in range(4):
        loads.main(3, (1 + block, block))
        loads.down(1, 5 + block, block)
    done = lambda slot: None
    step(2)
    fill_mask(mask, info[0])
    for key in keys:
        key.wait()
    attend(q_in, kv, info[0], attended, logs, step)
    wait(0)
    residual = hidden[...].astype(F32) + dot(attended[...], kept[0]) + main_bias[2:3, 2 * D : 3 * D]
    mid, norm, scale_mid = norm_forward(residual, gains[2:3, :], main_bias[2:3, 3 * D :])
    mid_out[...] = mid
    norm_a[...] = norm
    hidden_now = mid_out[...]
    total = feed_forward(
        hidden_now, main_bias[3:4, :], (1, 2, 3, 4), (5, 6, 7, 8), kept, act, slope, wait, step
    )
    residual = mid_out[...].astype(F32) + total + down_bias[2:3, :]
    out, norm, scale = norm_forward(residual, gains[3:4, :], down_bias[3:4, :])
    out_out[...] = out
    grad_float = cotangent[...].astype(F32)
    grad_now = norm_backward(grad_float, norm.astype(F32), scale, gains[3:4, :])
    terms[8:9, :] = jnp.sum(grad_now, axis=0, keepdims=True)
    terms[9:10, :] = jnp.sum(grad_float, axis=0, keepdims=True)
    total = feed_backward(
        grad_now.astype(BF16), slope, (1, 2, 3, 4), (5, 6, 7, 8), kept, act, terms, done, step
    )
    ig_out[...] = (grad_now + total).astype(BF16)
    start_attention_backward(
        ig_out[...], norm_a[...], scale_mid, gains[2:3, :], kept[0], grad_res, attended, terms
    )
    attend_backward(attended, q_in, kv, logs, mask, dq, dkv)
    finish_attention_backward(info[1], dq, dkv, dq_out, own_out, other_out, terms)


def input_grad(grad_res, dq_in, own_in, recv_in, kept, slots, wait, step):
    wait(slots[0])
    step()
    total = grad_res[...] + dot(dq_in[...], kept[slots[0]], NT)
    grads = (own_in[...].astype(F32) + recv_in[...].astype(F32)).astype(BF16)
    wait(slots[1])
    step()
    total = total + dot(grads[:, :D], kept[slots[1]], NT)
    wait(slots[2])
    step()
    return (total + dot(grads[:, D:], kept[slots[2]], NT)).astype(BF16)


def back_kernel(
    n_main, place, info, grad_in, dq_in, own_in, recv_in, gains, scale_f, scale_a, logs, high_terms, norm_f, slope,
    norm_a, q_in, kv_own, kv_other, w_down, *refs
):
    sources = refs[:n_main]
    (
        ig_high, ig_out, dq_out, own_out, other_out, grad_res, all_terms,
        kept, sems, kv, kv_sems, grad_att, act, mask, dq, dkv, slope_in, rows_in, row_sems,
    ) = refs[n_main:]
    keys = gather_keys(kv_own, kv_other, info[1], kv, kv_sems)
    terms = all_terms.at[0]
    all_terms[1] = high_terms[...]
    slope_copy = pltpu.make_async_copy(slope, slope_in, row_sems.at[3])
    copies = [
        pltpu.make_async_copy(array, rows_in.at[i], row_sems.at[i])
        for i, array in enumerate((norm_f, norm_a, q_in))
    ]
    loads = Loads(place, sources, w_down, kept, sems)
    wait, step = (loads.wait, loads.step)
    loads.main(2, (9, 0), (10, 1), (11, 2))
    loads.copies(copies[0], slope_copy)
    loads.down(0, 5, 0)
    loads.main(1, (1, 0))
    for block in (1, 2, 3):
        loads.down(0, 5 + block, block)
        loads.main(1, (1 + block, block))
    loads.main(0, (0, 3))
    loads.copies(*keys, *copies[1:])
    step(3)
    fill_mask(mask, info[0])
    step()
    ig_high[...] = input_grad(grad_in, dq_in, own_in, recv_in, kept, (9, 10, 11), wait, step)
    grad_float = ig_high[...].astype(F32)
    copies[0].wait()
    grad_now = norm_backward(grad_float, rows_in[0].astype(F32), scale_f[:, 0:1], gains[1:2, :])
    terms[8:9, :] = jnp.sum(grad_now, axis=0, keepdims=True)
    terms[9:10, :] = jnp.sum(grad_float, axis=0, keepdims=True)
    slope_copy.wait()
    total = feed_backward(
        grad_now.astype(BF16), slope_in, (1, 2, 3, 4), (5, 6, 7, 8), kept, act, terms, wait, lambda: step(2)
    )
    ig_out[...] = (grad_now + total).astype(BF16)
    step(8)
    wait(0)
    for copy in (*keys, *copies[1:]):
        copy.wait()
    start_attention_backward(
        ig_out[...], rows_in[1], scale_a[:, 0:1], gains[0:1, :], kept[0], grad_res, grad_att, terms
    )
    attend_backward(grad_att, rows_in.at[2], kv, logs, mask, dq, dkv)
    finish_attention_backward(info[1], dq, dkv, dq_out, own_out, other_out, terms)


def last_kernel(n_main, place, info, grad_res, dq_in, own_in, recv_in, ig_one, ig_two, ig_three, w_down, *refs):
    sources = refs[:n_main]
    *outs, kept, sems = refs[n_main:]
    loads = Loads(place, sources, w_down, kept, sems)
    loads.main(0, (0, 0), (1, 1), (2, 2))
    loads.step(3)
    for section, grads in ((1, ig_one), (2, ig_two), (3, ig_three)):
        for bits, out in enumerate(outs):

            @pl.when(info[2] == section ^ bits)
            def _():
                out[...] = grads[...]

    grads = input_grad(grad_res, dq_in, own_in, recv_in, kept, (0, 1, 2), loads.wait, loads.step)
    for bits, out in enumerate(outs):

        @pl.when(info[2] == bits)
        def _():
            out[...] = grads


def launch(kernel, name, work, outs, scratch, smem, vmem, hbm):
    return pl.pallas_call(
        functools.partial(kernel, len(hbm[1])),
        name=name,
        out_shape=outs,
        in_specs=[IN_SMEM] * len(smem)
        + [IN_VMEM] * len(vmem)
        + [IN_HBM] * (len(hbm[0]) + len(hbm[1])),
        out_specs=[IN_VMEM] * len(outs),
        scratch_shapes=scratch,
        cost_estimate=pl.CostEstimate(flops=int(work * 1e9), bytes_accessed=2**20, transcendentals=0),
        compiler_params=pltpu.CompilerParams(vmem_limit_bytes=58 * 2**20),
    )(*smem, *vmem, *hbm[0], *hbm[1])


def main_slots(count):
    return [pltpu.VMEM((count, D, D), BF16), pltpu.SemaphoreType.DMA((count,))]


def flip(value, axis, bit):
    count = lax.axis_size(axis)
    return lax.ppermute(value, axis, [(source, source ^ bit) for source in range(count)])


def tied(value, *others):
    return lax.optimization_barrier((value, *others))[0]


def split_three(value):
    high = lax.optimization_barrier(value.astype(BF16))
    rest = value - high.astype(F32)
    middle = lax.optimization_barrier(rest.astype(BF16))
    low = (rest - middle.astype(F32)).astype(BF16)
    return jnp.concatenate([high.reshape(-1, D), middle.reshape(-1, D), low.reshape(-1, D)])


def join_three(rows):
    parts = rows.astype(F32).reshape(3, -1)
    return parts[0] + parts[1] + parts[2]


def tied(values, *others):
    return lax.optimization_barrier((*values, *others))[: len(values)]


def gather_weights(own, base, small, early, finish):
    over_x = lambda value: flip(value, "section", 1)
    over_y = lambda value: flip(value, "section", 2)
    over_z = lambda value: flip(value, "dp", 2)
    over_core = lambda value: flip(value, "dp", 1)
    first = lax.dynamic_slice(own, (0, base * D), (ONE, D))
    second = lax.dynamic_slice(own, (ONE - EXTRA, base * D), (EXTRA + TWO, D))
    extra = split_three(small)
    rows = extra.shape[0]
    second = lax.dynamic_update_slice(lax.optimization_barrier(second), extra, (0, 0))
    far = lax.dynamic_slice(own, (ONE + MIDDLE, (base ^ 1) * D), (LATE, D))
    x_one, y_one, x_two = (over_x(first), over_y(first), over_x(second))
    y_two = over_y(jnp.concatenate([second, far]))
    early = early(first)

    x_first, y_first = tied((x_one, y_one))
    xz_one, d_one = (over_z(x_first), over_x(y_first))
    ones = jnp.concatenate([x_first, y_first])

    x_second, z_now, ones = tied((x_two, xz_one, ones), *early)
    dz_one, xz_two, c_ones = (over_y(z_now), over_z(x_second[EXTRA:]), over_core(ones))
    mixed = jnp.concatenate([x_second, z_now])

    y_second = y_two
    rest = jnp.concatenate([y_first, y_second[EXTRA : EXTRA + MIDDLE]])
    d_now, dz_now, xz_now, y_second, rest, mixed = tied((d_one, dz_one, xz_two, y_second, rest, mixed), c_ones)
    dz_two, yz, d_two = (over_y(xz_now), over_z(rest), over_x(y_second[: EXTRA + TWO]))
    c_mixed, yc_two = (over_core(mixed), over_core(y_second))

    two_now, dz_last, z_now, d_now, dz_now, xz_now = tied(
        (d_two, dz_two, yz, d_now, dz_now, xz_now), c_mixed, yc_two
    )
    dc_one, dzc_one, xzc_two = (over_core(d_now), over_core(dz_now), over_core(xz_now))
    dc_two, dzc_two, yzc = (over_core(two_now), over_core(dz_last), over_core(z_now))
    smalls = jnp.stack([small] + [join_three(piece[:rows]) for piece in (x_two, y_two, two_now)])
    smalls = finish(smalls)
    received = (
        x_one, x_two, xz_one, xz_two, c_ones, c_mixed, xzc_two, y_one, y_two, yz, yc_two, yzc,
        d_one, d_two, dz_one, dz_two, dc_one, dc_two, dzc_one, dzc_two,
    )
    return (list(received), smalls, early)


def butterfly_steps():
    steps = {}
    for axis in ("dp", "section"):
        bits = []
        while 2 ** len(bits) < lax.axis_size(axis):
            bits.append(2 ** len(bits))
        steps[axis] = [(axis, bit) for bit in bits]
    return steps["dp"][:1] + steps["section"][:1] + steps["dp"][1:] + steps["section"][1:]


def choose(values, index):
    low = jnp.where(index % 2 == 0, values[0], values[1])
    high = jnp.where(index % 2 == 0, values[2], values[3])
    return jnp.where(index < 2, low, high)


def pick(stack, index):
    return lax.dynamic_index_in_dim(stack, index, 0, keepdims=False)


def spread(mine, got_x, got_y, got_d, section, core):
    same = core == section % 2
    keep_first = jnp.where(same, mine, got_x)
    keep_second = jnp.where(same, got_y, got_d)
    send = jnp.stack([jnp.where(same, got_x, mine), jnp.where(same, got_d, got_y)])
    got = flip(send, "dp", 1)
    batch = section // 2
    kept_rows = [jnp.where(batch == 0, keep_first, keep_second), jnp.where(batch == 0, keep_second, keep_first)]
    got_rows = [jnp.where(batch == 0, got[0], got[1]), jnp.where(batch == 0, got[1], got[0])]
    parts = []
    for kept_now, got_now in zip(kept_rows, got_rows):
        parts.append(
            jnp.concatenate(
                [jnp.where(core == 0, kept_now, got_now), jnp.where(core == 0, got_now, kept_now)]
            )
        )
    return jnp.stack(parts)[None, :, None]


def per_device(inputs_x, lengths, w_main, w_down, gains, bias_main, bias_down, cotangent):
    section = lax.axis_index("section")
    lane = lax.axis_index("dp")
    core, plane = (lane % 2, (lane // 2) % 2)
    base = core * 2 + plane
    rows = inputs_x.shape[2] // 2

    batch = section // 2
    same = core == section % 2
    blocks = jnp.arange(4, dtype=jnp.int32)[None, :]
    away = section ^ jnp.arange(4, dtype=jnp.int32)[:, None]

    def take_inputs(after):
        tied_x, tied_grad, tied_lengths, _ = lax.optimization_barrier((inputs_x, cotangent, lengths, after))
        lines = jnp.stack([pick(tied_x[:, 0], batch), pick(tied_grad[:, 0], batch)])
        mine = lax.dynamic_slice_in_dim(lines, core * rows, rows, axis=1)
        other = flip(lax.dynamic_slice_in_dim(lines, (1 - core) * rows, rows, axis=1), "dp", 1)
        mine = jnp.where(same, mine, other)
        length_own = lax.dynamic_slice_in_dim(tied_lengths[:, 0], batch, 1).astype(F32)
        length_other = flip(jnp.broadcast_to(length_own[None], (8, 128)), "dp", 1)[0, :1]
        length = jnp.where(same, length_own, length_other).astype(jnp.int32)
        info = jnp.concatenate([length, core[None].astype(jnp.int32), section[None].astype(jnp.int32)])
        place = jnp.where(away == 0, 0, 1 + (away - 1) * 4 + (blocks ^ base)).astype(jnp.int32)
        return (mine[0], mine[1], info, place)

    small = jnp.concatenate([gains, bias_main], axis=1).reshape(-1)
    own = w_main[0]

    def take_smalls(smalls):
        smalls = jnp.stack([pick(smalls, section ^ s) for s in range(4)])
        return (smalls[:, :D], smalls[:, D:], bias_down.reshape(4, D))

    received, smalls, early = gather_weights(own, base, small, take_inputs, take_smalls)
    hidden, grad_last, info, place = early
    all_gains, all_bias, down_bias = smalls
    sources = [own] + received

    def row(width, kind):
        return SHAPE((rows, width), kind)

    pair_sems = pltpu.SemaphoreType.DMA((2,))
    keys = pltpu.VMEM((2 * rows, 2 * D), BF16)
    q0, kv0 = launch(
        first_kernel, "first", 5, [row(D, BF16), row(2 * D, BF16)], main_slots(3),
        [place], [hidden, all_bias], ([w_down], sources),
    )
    kv0_other = flip(kv0, "dp", 1)
    hs0, hs1, q2, kv2, logs0, norm0, scale0, norm1, scale1, slope1 = launch(
        low_kernel, "low", 20,
        [
            row(D, BF16), row(D, BF16), row(D, BF16), row(2 * D, BF16), SHAPE((128, rows), F32),
            row(D, BF16), row(128, F32), row(D, BF16), row(128, F32), row(FF, BF16),
        ],
        main_slots(12)
        + [keys, pair_sems, pltpu.VMEM((rows, D), BF16), pltpu.VMEM((rows, FF), BF16)],
        [place, info], [hidden, q0, all_bias, down_bias, all_gains, kv0, kv0_other], ([w_down], sources),
    )
    kv2_other = flip(kv2, "dp", 1)
    hs2, hs3, ig3, dq2, own2, other2, res2, terms2 = launch(
        high_kernel, "high", 32,
        [
            row(D, BF16), row(D, BF16), row(D, BF16), row(D, BF16), row(2 * D, BF16), row(2 * D, BF16),
            row(D, F32), SHAPE((10, D), F32),
        ],
        main_slots(9)
        + [
            keys, pair_sems, pltpu.VMEM((rows, D), BF16), pltpu.VMEM((rows, FF), BF16),
            pltpu.VMEM((rows, FF), BF16), pltpu.VMEM((2 * rows, rows), F32), pltpu.VMEM((128, rows), F32),
            pltpu.VMEM((rows, D), BF16), pltpu.VMEM((rows, D), F32), pltpu.VMEM((2 * rows, 2 * D), F32),
        ],
        [place, info], [hs1, q2, grad_last, all_bias, down_bias, all_gains, kv2, kv2_other],
        ([w_down], sources),
    )
    recv2 = flip(other2, "dp", 1)
    ig2, ig1, dq0, own0, other0, res0, terms = launch(
        back_kernel, "back", 20,
        [
            row(D, BF16), row(D, BF16), row(D, BF16), row(2 * D, BF16), row(2 * D, BF16), row(D, F32),
            SHAPE((2, 10, D), F32),
        ],
        main_slots(12)
        + [
            keys, pair_sems, pltpu.VMEM((rows, D), BF16), pltpu.VMEM((rows, FF), BF16),
            pltpu.VMEM((2 * rows, rows), F32), pltpu.VMEM((rows, D), F32), pltpu.VMEM((2 * rows, 2 * D), F32),
            pltpu.VMEM((rows, FF), BF16), pltpu.VMEM((3, rows, D), BF16), pltpu.SemaphoreType.DMA((4,)),
        ],
        [place, info],
        [res2, dq2, own2, recv2, all_gains, scale1, scale0, logs0, terms2],
        ([norm1, slope1, norm0, q0, kv0, kv0_other, w_down], sources),
    )
    outputs = [choose((hs0, hs1, hs2, hs3), section ^ bits) for bits in range(4)]
    outputs = [outputs[0]] + [flip(outputs[bits], "section", bits) for bits in (1, 2, 3)]
    other0, terms, res0, *outputs = tied((other0, terms, res0, *outputs))
    recv0 = flip(other0, "dp", 1)
    core_step, first_step, *middle_steps = butterfly_steps()
    terms = terms + flip(terms, *core_step)
    got = flip(terms, *first_step)
    grads = launch(
        last_kernel, "last", 5, [row(D, BF16)] * 4, main_slots(3), [place, info],
        [res0, dq0, own0, recv0, ig1, ig2, ig3], ([w_down], sources),
    )
    terms, got, *grads = tied((terms, got, *grads))
    terms = terms + got
    moved = [flip(grads[bits], "section", bits) for bits in (1, 2, 3)]
    for axis, bit in middle_steps:
        terms = terms + flip(terms, axis, bit)
    terms, *moved = tied((terms, *moved))
    hidden_states = spread(*outputs, section, core)
    input_grads = spread(grads[0], *moved, section, core)
    grad_main = terms[:, :8].reshape(4, FF)
    return (hidden_states, input_grads, grad_main, terms[:, 8:])


def solution(mesh):
    placed = (
        P(None, "dp", None, None),
        P(None, "dp"),
        P("section", None, None),
        P(),
        P("section", None),
        P("section", None),
        P(),
        P(None, "dp", None, None),
    )
    return jax.shard_map(
        per_device,
        mesh=mesh,
        in_specs=placed,
        out_specs=(
            P("section", None, "dp", None, None),
            P("section", None, "dp", None, None),
            P(),
            P(),
        ),
        check_vma=False,
    )
```
